512 devices in a mesh: inner: 16 (over x_hi, y, core), outer: 32 (over x_lo, z).
Axes of the slice: x: 4 (x_hi: 2, x_lo: 2; x = x_hi * 2 + x_lo), y: 4, z: 16, core: 2. Of those that a mesh axis runs over, the one named last changes fastest.
Arguments:
- queries: bfloat16 [65536, 4096], P(('inner', 'outer')), may hold values from -41 to 41
- key_states: bfloat16 [65536, 512], P(('inner', 'outer')), may hold values from -4 to 4
- value_states: bfloat16 [65536, 512], P(('inner', 'outer')), may hold values from -6 to 6
- out_grad: bfloat16 [65536, 4096], P(('inner', 'outer')), may hold values from -6 to 6
- segment_ids: int32 [65536], P(('inner', 'outer')), may hold values from 0 to 511, never falling along the last dimension, each value on 1 to 256 neighbouring positions
Outputs:
- query_grad: bfloat16 [65536, 4096], P(('inner', 'outer'))
- key_grad: bfloat16 [65536, 512], P(('inner', 'outer'))
- value_grad: bfloat16 [65536, 512], P(('inner', 'outer'))
The draws below stay inside these ranges and needn't reach their ends.
Inputs may be any that keep to these rules, and one draw needn't show every extreme that they name: `segment_ids`: ids never fall along the tokens; every document has 1 to 256 tokens, and one has exactly that many.
All inputs are finite; a program needn't handle non-finite values.
Results may differ from the reference program's by a relative error of at most 0.025.
Values may be sent and summed in bfloat16 or wider, within the bound.
No kernel may reach another device: no remote copies, remote signals or barrier semaphores. Data moves between devices by JAX's collectives and lax.ppermute only.
A program may use at most 64 MiB of HBM per device.

```python
import math
import jax
import jax.numpy as jnp
import numpy as np
from jax import lax

HQ = 32
HK = 4
HD = 128
TOK_DEV = 128
REACH = 2
TOKENS = 65536
DOCS = 512


def common_keys(key):
    return jax.random.normal(key, (TOKENS, HK * HD), jnp.float32)


def draw_key_states(key, part):
    base = common_keys(key)
    values = jnp.clip(base, -4.0, 4.0)
    return values.astype(jnp.bfloat16)


def draw_queries(key, part):
    key = jax.random.fold_in(key, 23)
    noise_key = jax.random.fold_in(key, 0)
    values = jnp.clip(jax.random.normal(noise_key, (TOKENS, HQ * HD), jnp.float32), -4.0, 4.0)
    return values.astype(jnp.bfloat16)


def shard_levels(rng, shape, shards, smallest, largest):
    factor_of, own = 1.0, jax.random.fold_in(rng, 6)
    for position, parts in shards:
        draws = jnp.exp(jax.random.uniform(jax.random.fold_in(own, position), (parts,), jnp.float32, smallest / len(shards), largest / len(shards)))
        factor_of = factor_of * jnp.repeat(draws, shape[position] // parts).reshape([-1 if axis == position else 1 for axis in range(len(shape))])
    return factor_of


def split_up(number_of, total, limit, slope):
    portions = [(1 << 20) // math.isqrt(standing ** slope) + 1 for standing in range(2, number_of + 1)]
    spare, counts = total - limit - (number_of - 1), [1] * (number_of - 1)
    while spare > 0:
        free = [i for i in range(number_of - 1) if counts[i] < limit]
        whole, left = sum([portions[i] for i in free]), spare
        for i in free:
            addition = min(limit - counts[i], max(1, left * portions[i] // whole), spare)
            counts[i] = counts[i] + addition
            spare = spare - addition
    return np.array([limit] + counts)


def ragged(rng, number_of, total, limit, slope):
    if number_of == 2:
        one = jax.random.randint(rng, (), max(1, total - limit), min(limit, total - 1) + 1)
        return jnp.stack([one, total - one])
    tallies = jnp.asarray(split_up(number_of, total, limit, slope), jnp.int32)
    couples = (number_of - 1) // 2
    source_of, receiver = tallies[1:1 + 2 * couples:2], tallies[2:2 + 2 * couples:2]
    room = jnp.minimum(source_of - 1, limit - receiver)
    moved = jax.random.randint(jax.random.fold_in(rng, 1), (couples,), 0, 1 << 20) % (room + 1)
    tallies = tallies.at[1:1 + 2 * couples:2].set(source_of - moved).at[2:2 + 2 * couples:2].set(receiver + moved)
    return tallies[jax.random.permutation(jax.random.fold_in(rng, 2), number_of)]


def centred(stream_key, shape, scale, reach, pieces=(), held_as=jnp.bfloat16):
    loudness = shard_levels(stream_key, shape, pieces, -0.22, 0.18) if pieces else 1.0
    values = jax.random.normal(stream_key, shape, jnp.float32) * scale * loudness
    return jnp.minimum(jnp.maximum(values, -reach), reach).astype(held_as)


def setup_inputs(seed: int = 0) -> dict:
    seeds = jax.random.split(jax.random.key(seed), 6)
    queries = draw_queries(jax.random.fold_in(seeds[5], 71), 0)
    key_states = draw_key_states(jax.random.fold_in(seeds[5], 71), 0)
    value_states = centred(seeds[2], (TOKENS, HK * HD), 1.0, 6.0, ((0, 512),))
    out_grad = centred(seeds[3], (TOKENS, HQ * HD), 1.0, 6.0, ((0, 512),))
    segment_ids = jnp.searchsorted(jnp.cumsum(ragged(seeds[4], DOCS, TOKENS, REACH * TOK_DEV, 0)), jnp.arange(TOKENS), side="right").astype(jnp.int32)
    return dict(queries=queries, key_states=key_states, value_states=value_states, out_grad=out_grad, segment_ids=segment_ids)


NEG = -1e30


def reference(queries, key_states, value_states, out_grad, segment_ids):
    total = queries.shape[0]
    group = HQ // HK
    scale = HD ** -0.5
    width = (REACH + 1) * TOK_DEV
    margin = REACH * TOK_DEV
    keys = jnp.concatenate([jnp.zeros((margin, HK * HD), key_states.dtype), key_states]).reshape(-1, HK, HD)
    values = jnp.concatenate([jnp.zeros((margin, HK * HD), value_states.dtype), value_states]).reshape(-1, HK, HD)
    segs = jnp.concatenate([jnp.full((margin,), -1, jnp.int32), segment_ids.astype(jnp.int32)])
    blocks = total // TOK_DEV
    q_all = queries.reshape(blocks, TOK_DEV, HK, group, HD)
    g_all = out_grad.reshape(blocks, TOK_DEV, HK, group, HD)
    s_all = segment_ids.reshape(blocks, TOK_DEV)
    qpos = jnp.arange(TOK_DEV, dtype=jnp.int32) + margin
    kpos = jnp.arange(width, dtype=jnp.int32)

    def step(carry, inputs):
        dk_all, dv_all = carry
        index, q_blk, g_blk, s_blk = inputs
        start = (index * TOK_DEV).astype(jnp.int32)
        k_win = lax.dynamic_slice_in_dim(keys, start, width, 0).astype(jnp.float32)
        v_win = lax.dynamic_slice_in_dim(values, start, width, 0).astype(jnp.float32)
        seg_win = lax.dynamic_slice_in_dim(segs, start, width, 0)
        qf = q_blk.astype(jnp.float32)
        gf = g_blk.astype(jnp.float32)
        scores = jnp.einsum("tkgd,wkd->kgtw", qf, k_win) * scale
        allowed = (s_blk[:, None] == seg_win[None, :]) & (kpos[None, :] <= qpos[:, None])
        masked = jnp.where(allowed, scores, NEG)
        top = jnp.max(masked, -1)
        total_exp = jnp.sum(jnp.where(allowed, jnp.exp(masked - top[..., None]), 0.0), -1)
        lse = top + jnp.log(total_exp)
        probs = jnp.where(allowed, jnp.exp(scores - lse[..., None]), 0.0)
        probs_low = lax.optimization_barrier(probs.astype(jnp.bfloat16)).astype(jnp.float32)
        attended = jnp.einsum("kgtw,wkd->tkgd", probs_low, v_win).astype(jnp.bfloat16)
        delta = jnp.transpose(jnp.sum(gf * attended.astype(jnp.float32), -1), (1, 2, 0))
        dprobs = jnp.einsum("tkgd,wkd->kgtw", gf, v_win)
        dscores = lax.optimization_barrier((probs * (dprobs - delta[..., None])).astype(jnp.bfloat16)).astype(jnp.float32)
        dq = (jnp.einsum("kgtw,wkd->tkgd", dscores, k_win) * scale).astype(jnp.bfloat16)
        dk = jnp.einsum("kgtw,tkgd->wkd", dscores, qf) * scale
        dv = jnp.einsum("kgtw,tkgd->wkd", probs_low, gf)
        dk_all = lax.dynamic_update_slice_in_dim(dk_all, lax.dynamic_slice_in_dim(dk_all, start, width, 0) + dk, start, 0)
        dv_all = lax.dynamic_update_slice_in_dim(dv_all, lax.dynamic_slice_in_dim(dv_all, start, width, 0) + dv, start, 0)
        return (dk_all, dv_all), dq

    zeros = jnp.zeros((total + margin, HK, HD), jnp.float32)
    indices = jnp.arange(blocks, dtype=jnp.int32)
    (dk_all, dv_all), dq = lax.scan(step, (zeros, zeros), (indices, q_all, g_all, s_all))
    query_grad = dq.reshape(total, HQ * HD)
    key_grad = dk_all[margin:].reshape(total, HK * HD).astype(jnp.bfloat16)
    value_grad = dv_all[margin:].reshape(total, HK * HD).astype(jnp.bfloat16)
    return query_grad, key_grad, value_grad
```

```python
import functools

import jax
import jax.numpy as jnp
from jax import lax
from jax.experimental import pallas as pl
from jax.experimental.pallas import tpu as pltpu
from jax.sharding import PartitionSpec as P

HK = 4
HD = 128
SEG_ROWS = 16
NEG = -1e30
LOG2E = 1.4426950408889634
AXES = ("inner", "outer")
CHUNKS = 2
VMEM_LIMIT = 24 * 1024 * 1024


def shift(value, steps):
    count = lax.axis_size(AXES)
    first, last = max(0, -steps), min(count, count - steps)
    return lax.ppermute(value, AXES, [(i, i + steps) for i in range(first, last)])


def dot(a, b):
    return jnp.dot(a, b, preferred_element_type=jnp.float32)


def stacked(ref, first, count):
    return jnp.concatenate(
        [ref[:, (first + h) * HD : (first + h + 1) * HD] for h in range(count)], axis=0
    )


def sees_own(tokens, copies):
    key = lax.broadcasted_iota(jnp.int32, (tokens, tokens), 0)
    query = lax.broadcasted_iota(jnp.int32, (tokens, tokens), 1)
    return jnp.concatenate([key <= query] * copies, axis=1)


def segments(ref, tokens):
    coded = ref[2 * tokens : 2 * tokens + SEG_ROWS, :].astype(jnp.float32)
    row = coded[0:1] * 2.0 + coded[1:2]
    return jnp.broadcast_to(row, (tokens, tokens))


def pack_kernel(tokens, k_ref, v_ref, seg_ref, *refs):
    out_refs, seg_own, sems = refs[:-2], refs[-2], refs[-1]
    width = k_ref.shape[1] // len(out_refs)
    ids = pltpu.make_async_copy(seg_ref, seg_own, sems.at[0])
    ids.start()
    copies = []
    for index, out_ref in enumerate(out_refs):
        cols = pl.ds(index * width, width)
        for half, source in enumerate((k_ref, v_ref)):
            copies.append(
                pltpu.make_async_copy(
                    source.at[:, cols], out_ref.at[pl.ds(half * tokens, tokens), :],
                    sems.at[1 + 2 * index + half],
                )
            )
    for copy in copies:
        copy.start()
    ids.wait()
    seg = jnp.broadcast_to((seg_own[...] + 1)[None, :], (SEG_ROWS, tokens))
    row = lax.broadcasted_iota(jnp.int32, (SEG_ROWS, tokens), 0)
    coded = jnp.where(row == 0, seg >> 1, jnp.where(row == 1, seg & 1, 0))
    coded = coded.astype(jnp.float32).astype(jnp.bfloat16)
    for out_ref in out_refs:
        out_ref[2 * tokens : 2 * tokens + SEG_ROWS, :] = jnp.concatenate([coded] * (width // tokens), axis=1)
    for copy in copies:
        copy.wait()


def turn_kernel(q_ref, g_ref, qt_ref, gt_ref):
    for h in range(q_ref.shape[1] // HD):
        cols = slice(h * HD, (h + 1) * HD)
        qt_ref[:, cols] = jnp.transpose(q_ref[:, cols])
        gt_ref[:, cols] = jnp.transpose(g_ref[:, cols])


def score_kernel(group, tokens, scale, q_ref, g_ref, qt_ref, gt_ref, own_ref, one_ref, two_ref,
                 p_ref, ds_ref, far_ref, near_ref, bias_ref):
    @pl.when(pl.program_id(0) == 0)
    def _():
        seg_query = segments(own_ref, tokens)
        seg_own = jnp.transpose(seg_query)
        seg_one = jnp.transpose(segments(one_ref, tokens))
        seg_two = jnp.transpose(segments(two_ref, tokens))
        mixed = jnp.where(sees_own(tokens, 1), seg_own, seg_two)
        bias_ref[0:tokens, :] = jnp.where(mixed == seg_query, 0.0, NEG)
        bias_ref[tokens : 2 * tokens, :] = jnp.where(seg_one == seg_query, 0.0, NEG)

    tri = sees_own(tokens, 2)
    own_mask = jnp.where(tri, 1.0, 0.0).astype(jnp.bfloat16)
    far_mask = jnp.where(tri, 0.0, 1.0).astype(jnp.bfloat16)
    bias_mix = jnp.concatenate([bias_ref[0:tokens, :]] * 2, axis=1)
    bias_one = jnp.concatenate([bias_ref[tokens : 2 * tokens, :]] * 2, axis=1)
    keys = jnp.concatenate([own_ref[0:tokens, :], one_ref[0:tokens, :], two_ref[0:tokens, :]], axis=0)
    vals = jnp.concatenate(
        [own_ref[tokens : 2 * tokens, :], one_ref[tokens : 2 * tokens, :], two_ref[tokens : 2 * tokens, :]],
        axis=0,
    )
    factor = scale * LOG2E
    sum_k = jnp.zeros((2 * tokens, HD), jnp.float32)
    sum_v = jnp.zeros((2 * tokens, HD), jnp.float32)
    pairs = group // 2
    spans = [slice(pair * 2 * HD, (pair + 1) * 2 * HD) for pair in range(pairs)]
    products = [(dot(keys, qt_ref[:, spans[0]]), dot(vals, gt_ref[:, spans[0]]))]
    for pair, cols in enumerate(spans):
        if pair + 1 < pairs:
            products.append((dot(keys, qt_ref[:, spans[pair + 1]]), dot(vals, gt_ref[:, spans[pair + 1]])))
        raw, dp = products[pair]
        s_mix = jnp.where(tri, raw[0:tokens], raw[2 * tokens :]) + bias_mix
        s_one = raw[tokens : 2 * tokens] + bias_one
        top = jnp.max(jnp.maximum(s_mix, s_one), axis=0, keepdims=True)
        e_mix = jnp.exp2((s_mix - top) * factor)
        e_one = jnp.exp2((s_one - top) * factor)
        inverse = 1.0 / jnp.sum(e_mix + e_one, axis=0, keepdims=True)
        p_mix = e_mix * inverse
        p_one = e_one * inverse
        d_mix = jnp.where(tri, dp[0:tokens], dp[2 * tokens :])
        d_one = dp[tokens : 2 * tokens]
        delta = jnp.sum(p_mix * d_mix + p_one * d_one, axis=0, keepdims=True)
        ds_mix = (p_mix * (d_mix - delta)).astype(jnp.bfloat16)
        ds_one = (p_one * (d_one - delta)).astype(jnp.bfloat16)
        p_mix = p_mix.astype(jnp.bfloat16)
        p_one = p_one.astype(jnp.bfloat16)
        p_ref[:, cols] = p_mix * own_mask
        ds_ref[0:tokens, cols] = ds_mix
        ds_ref[tokens : 2 * tokens, cols] = ds_one
        sum_k = sum_k + dot(jnp.concatenate([ds_one, ds_mix * far_mask], axis=0), stacked(q_ref, 2 * pair, 2))
        sum_v = sum_v + dot(jnp.concatenate([p_one, p_mix * far_mask], axis=0), stacked(g_ref, 2 * pair, 2))
    near_ref[0:tokens, :] = sum_k[0:tokens] * scale
    near_ref[tokens : 2 * tokens, :] = sum_v[0:tokens]
    far_ref[0:tokens, :] = (sum_k[tokens:] * scale).astype(far_ref.dtype)
    far_ref[tokens : 2 * tokens, :] = sum_v[tokens:].astype(far_ref.dtype)


def rest_kernel(group, tokens, scale, p_ref, ds_ref, q_ref, g_ref, own_ref, one_ref, two_ref, *refs):
    dq_ref, own_out = refs[-2:]
    far_ref = refs[0] if len(refs) > 2 else None
    tri = sees_own(tokens, 2)
    own_mask = jnp.where(tri, 1.0, 0.0).astype(jnp.bfloat16)
    far_mask = jnp.where(tri, 0.0, 1.0).astype(jnp.bfloat16)

    def flipped(ref):
        return jnp.transpose(ref[0:tokens, :].astype(jnp.float32)).astype(jnp.bfloat16)

    keys_t = jnp.concatenate([flipped(own_ref), flipped(one_ref), flipped(two_ref)], axis=1)
    sum_k = jnp.zeros((tokens, HD), jnp.float32)
    sum_v = jnp.zeros((tokens, HD), jnp.float32)
    for pair in range(group // 2):
        cols = slice(pair * 2 * HD, (pair + 1) * 2 * HD)
        ds_mix = ds_ref[0:tokens, cols]
        ds_own = ds_mix * own_mask
        sum_k = sum_k + dot(ds_own, stacked(q_ref, 2 * pair, 2))
        sum_v = sum_v + dot(p_ref[:, cols], stacked(g_ref, 2 * pair, 2))
        rows = jnp.concatenate([ds_own, ds_ref[tokens : 2 * tokens, cols], ds_mix * far_mask], axis=0)
        dq_t = dot(keys_t, rows) * scale
        for h in range(2):
            head = dq_t[:, h * HD : (h + 1) * HD]
            dq_ref[:, (2 * pair + h) * HD : (2 * pair + h + 1) * HD] = jnp.transpose(head).astype(dq_ref.dtype)
    sum_k = sum_k * scale
    if far_ref is not None:
        sum_k = sum_k + far_ref[0:tokens, :].astype(jnp.float32)
        sum_v = sum_v + far_ref[tokens : 2 * tokens, :].astype(jnp.float32)
    own_out[0:tokens, :] = sum_k
    own_out[tokens : 2 * tokens, :] = sum_v


def join_kernel(first_ref, handed_ref, second_ref, out_ref):
    width = first_ref.shape[1]
    out_ref[:, 0:width] = (first_ref[...] + handed_ref[...].astype(jnp.float32)).astype(out_ref.dtype)
    out_ref[:, width:] = second_ref[...].astype(out_ref.dtype)


def final_kernel(tokens, near_ref, *refs):
    k_out, v_out = refs[-2:]
    for index, own_ref in enumerate(refs[:-2]):
        width = own_ref.shape[1]
        cols = slice(index * width, (index + 1) * width)
        total = own_ref[...] + near_ref[:, cols].astype(jnp.float32)
        k_out[:, cols] = total[0:tokens].astype(k_out.dtype)
        v_out[:, cols] = total[tokens:].astype(v_out.dtype)


def column(rows, width, offset=0):
    return pl.BlockSpec((rows, width), lambda i: (0, i + offset))


def bf16(*shape):
    return jax.ShapeDtypeStruct(shape, jnp.bfloat16)


def f32(*shape):
    return jax.ShapeDtypeStruct(shape, jnp.float32)


def cost(flops, bytes_accessed, transcendentals=0):
    return pl.CostEstimate(flops=flops, bytes_accessed=bytes_accessed, transcendentals=transcendentals)


PARAMS = pltpu.CompilerParams(vmem_limit_bytes=VMEM_LIMIT)


def pack_call(key_states, value_states, segment_ids):
    tokens, width = key_states.shape
    operands = [pltpu.with_memory_space_constraint(x, pltpu.HBM) for x in (key_states, value_states, segment_ids)]
    return pl.pallas_call(
        functools.partial(pack_kernel, tokens),
        in_specs=[pl.BlockSpec(memory_space=pltpu.HBM)] * 3,
        out_shape=[bf16(2 * tokens + SEG_ROWS, width // CHUNKS) for _ in range(CHUNKS)],
        scratch_shapes=[
            pltpu.VMEM((tokens,), jnp.int32),
            pltpu.SemaphoreType.DMA((1 + 2 * CHUNKS,)),
        ],
        cost_estimate=cost(0, 8 * tokens * width),
        compiler_params=PARAMS,
        name="pack",
    )(*operands)


def turn_call(q, g):
    tokens, span = q.shape
    wide = span // HK
    return pl.pallas_call(
        turn_kernel,
        grid=(HK,),
        in_specs=[column(tokens, wide)] * 2,
        out_specs=[column(HD, wide)] * 2,
        out_shape=[bf16(HD, span)] * 2,
        cost_estimate=cost(0, 16 * tokens * span),
        compiler_params=PARAMS,
        name="turn",
    )(q, g)


def score_call(q, g, qt, gt, own, one, two, offset, group, tokens, scale):
    count = own.shape[1] // HD
    wide = group * HD
    span = count * wide
    payload = column(2 * tokens + SEG_ROWS, HD)
    return pl.pallas_call(
        functools.partial(score_kernel, group, tokens, scale),
        grid=(count,),
        in_specs=[column(tokens, wide, offset)] * 2 + [column(HD, wide, offset)] * 2 + [payload] * 3,
        out_specs=[column(tokens, wide), column(2 * tokens, wide), column(2 * tokens, HD), column(2 * tokens, HD)],
        out_shape=[
            bf16(tokens, span),
            bf16(2 * tokens, span),
            bf16(2 * tokens, count * HD),
            f32(2 * tokens, count * HD),
        ],
        scratch_shapes=[pltpu.VMEM((2 * tokens, tokens), jnp.float32)],
        cost_estimate=cost(2 * tokens * 3 * span * tokens * 4, 12 * tokens * span, 2 * tokens * span),
        compiler_params=PARAMS,
        name="scores",
    )(q, g, qt, gt, own, one, two)


def rest_call(p, ds, q, g, own, one, two, far, before, offset, group, tokens, scale):
    count = own.shape[1] // HD
    wide = group * HD
    payload = column(2 * tokens + SEG_ROWS, HD)
    operands = [p, ds, q, g, own, one, two]
    specs = [column(tokens, wide), column(2 * tokens, wide)] + [column(tokens, wide, offset)] * 2 + [payload] * 3
    aliases = {}
    if far is not None:
        operands.append(far)
        specs.append(column(2 * tokens, HD))
    if before is not None:
        aliases = {len(operands): 0}
        operands.append(before)
        specs.append(pl.BlockSpec(memory_space=pl.ANY))
    return pl.pallas_call(
        functools.partial(rest_kernel, group, tokens, scale),
        grid=(count,),
        in_specs=specs,
        out_specs=[column(tokens, wide, offset), column(2 * tokens, HD)],
        out_shape=[bf16(tokens, q.shape[1]), f32(2 * tokens, count * HD)],
        input_output_aliases=aliases,
        cost_estimate=cost(2 * tokens * 3 * count * wide * tokens * 2, 12 * tokens * count * wide),
        compiler_params=PARAMS,
        name="rest",
    )(*operands)


def join_call(first, handed, second):
    rows, width = first.shape
    return pl.pallas_call(
        join_kernel,
        out_shape=bf16(rows, 2 * width),
        cost_estimate=cost(0, 12 * rows * width),
        compiler_params=PARAMS,
        name="join",
    )(first, handed, second)


def final_call(near, owns):
    tokens, width = near.shape[0] // 2, near.shape[1]
    return pl.pallas_call(
        functools.partial(final_kernel, tokens),
        out_shape=[bf16(tokens, width)] * 2,
        cost_estimate=cost(0, 16 * tokens * width),
        compiler_params=PARAMS,
        name="final",
    )(near, *owns)


def shards(queries, key_states, value_states, out_grad, segment_ids):
    tokens = queries.shape[0]
    group = queries.shape[1] // (HK * HD)
    scale = HD ** (-0.5)
    chunks = range(CHUNKS)
    step = HK // CHUNKS
    own = pack_call(key_states, value_states, segment_ids)
    one = [shift(x, 1) for x in own]
    two = [shift(own[0], 2), shift(one[1], 1)]
    qt, gt = turn_call(queries, out_grad)
    first = [
        score_call(queries, out_grad, qt, gt, own[c], one[c], two[c], c * step, group, tokens, scale)
        for c in chunks
    ]
    handed = shift(first[0][2], -1)
    near = join_call(first[0][3], handed, first[1][3])
    near = shift(near, -1)
    far = [None, shift(first[1][2], -2)]
    query_grad, parts = None, []
    for c in chunks:
        query_grad, part = rest_call(
            first[c][0], first[c][1], queries, out_grad, own[c], one[c], two[c], far[c], query_grad,
            c * step, group, tokens, scale,
        )
        parts.append(part)
    key_grad, value_grad = final_call(near, parts)
    return query_grad, key_grad, value_grad


def solution(mesh):
    rows = P(AXES, None)
    return jax.shard_map(
        shards,
        mesh=mesh,
        in_specs=(rows, rows, rows, rows, P(AXES)),
        out_specs=(rows, rows, rows),
        check_vma=False,
    )
```

```python
import functools

import jax
import jax.numpy as jnp
from jax import lax
from jax.experimental import pallas as pl
from jax.experimental.pallas import tpu as pltpu
from jax.sharding import PartitionSpec as P

HK = 4
HD = 128
SEG_ROWS = 16
NEG = -1e30
LOG2E = 1.4426950408889634
AXES = ("inner", "outer")
CHUNKS = 2
VMEM_LIMIT = 24 * 1024 * 1024


def shift(value, steps):
    count = lax.axis_size(AXES)
    first, last = max(0, -steps), min(count, count - steps)
    return lax.ppermute(value, AXES, [(i, i + steps) for i in range(first, last)])


def dot(a, b):
    return jnp.dot(a, b, preferred_element_type=jnp.float32)


def stacked(ref, first, count):
    return jnp.concatenate(
        [ref[:, (first + h) * HD : (first + h + 1) * HD] for h in range(count)], axis=0
    )


def sees_own(tokens, copies):
    key = lax.broadcasted_iota(jnp.int32, (tokens, tokens), 0)
    query = lax.broadcasted_iota(jnp.int32, (tokens, tokens), 1)
    return jnp.concatenate([key <= query] * copies, axis=1)


def segments(payload, tokens):
    coded = payload[2 * tokens : 2 * tokens + SEG_ROWS, :].astype(jnp.float32)
    row = coded[0:1] * 2.0 + coded[1:2]
    return jnp.broadcast_to(row, (tokens, tokens))


def pack_kernel(tokens, k_ref, v_ref, seg_ref, *refs):
    out_refs, seg_own, sems = refs[:-2], refs[-2], refs[-1]
    width = k_ref.shape[1] // len(out_refs)
    ids = pltpu.make_async_copy(seg_ref, seg_own, sems.at[0])
    ids.start()
    copies = []
    for index, out_ref in enumerate(out_refs):
        cols = pl.ds(index * width, width)
        for half, source in enumerate((k_ref, v_ref)):
            copies.append(
                pltpu.make_async_copy(
                    source.at[:, cols], out_ref.at[pl.ds(half * tokens, tokens), :],
                    sems.at[1 + 2 * index + half],
                )
            )
    for copy in copies:
        copy.start()
    ids.wait()
    seg = jnp.broadcast_to((seg_own[...] + 1)[None, :], (SEG_ROWS, tokens))
    row = lax.broadcasted_iota(jnp.int32, (SEG_ROWS, tokens), 0)
    coded = jnp.where(row == 0, seg >> 1, jnp.where(row == 1, seg & 1, 0))
    coded = coded.astype(jnp.float32).astype(jnp.bfloat16)
    out_refs[0][2 * tokens : 2 * tokens + SEG_ROWS, :] = jnp.concatenate([coded] * (width // tokens), axis=1)
    for copy in copies:
        copy.wait()


def turn_kernel(q_ref, g_ref, q_out, g_out, qt_ref, gt_ref, sems):
    width = q_ref.shape[1] // HK
    copies = []
    for part in range(HK):
        cols = pl.ds(part * width, width)
        for side, (source, target) in enumerate(((q_ref, q_out), (g_ref, g_out))):
            copies.append(pltpu.make_async_copy(source.at[:, cols], target.at[:, cols], sems.at[2 * part + side]))
    for copy in copies:
        copy.start()
    for part in range(HK):
        for side, (source, target) in enumerate(((q_out, qt_ref), (g_out, gt_ref))):
            copies[2 * part + side].wait()
            for h in range(width // HD):
                cols = slice(part * width + h * HD, part * width + (h + 1) * HD)
                target[:, cols] = jnp.transpose(source[:, cols])


def score_kernel(group, tokens, scale, known, offset, q_ref, g_ref, qt_ref, gt_ref, own_ref, one_ref, two_ref,
                 *refs):
    p_ref, ds_ref, far_ref, near_ref = refs[1:] if known else refs[:-1]
    bias_ref = refs[0] if known else refs[-1]
    if known:
        bias = bias_ref[...]
    else:
        ids = slice(0, HD)
        seg_query = segments(own_ref[:, ids], tokens)
        seg_own = jnp.transpose(seg_query)
        seg_one = jnp.transpose(segments(one_ref[:, ids], tokens))
        seg_two = jnp.transpose(segments(two_ref[:, ids], tokens))
        mixed = jnp.where(sees_own(tokens, 1), seg_own, seg_two)
        bias = jnp.concatenate(
            [jnp.where(mixed == seg_query, 0.0, NEG), jnp.where(seg_one == seg_query, 0.0, NEG)], axis=0
        )
        bias_ref[...] = bias
    bias_mix = jnp.concatenate([bias[0:tokens]] * 2, axis=1)
    bias_one = jnp.concatenate([bias[tokens:]] * 2, axis=1)
    tri = sees_own(tokens, 2)
    far_mask = jnp.where(tri, 0.0, 1.0).astype(jnp.bfloat16)
    factor = scale * LOG2E
    pairs = group // 2
    count = own_ref.shape[1] // HD

    def products(unit):
        part, pair = divmod(unit, pairs)
        cols = slice(part * HD, (part + 1) * HD)
        keys, vals = [
            jnp.concatenate([ref[rows, cols] for ref in (own_ref, one_ref, two_ref)], axis=0)
            for rows in (slice(0, tokens), slice(tokens, 2 * tokens))
        ]
        first = (offset + part) * group + 2 * pair
        both = slice(first * HD, (first + 2) * HD)
        return dot(keys, qt_ref[:, both]), dot(vals, gt_ref[:, both])

    ahead = products(0)
    for part in range(count):
        sum_k = jnp.zeros((2 * tokens, HD), jnp.float32)
        sum_v = jnp.zeros((2 * tokens, HD), jnp.float32)
        for pair in range(pairs):
            unit = part * pairs + pair
            raw, dp = ahead
            if unit + 1 < count * pairs:
                ahead = products(unit + 1)
            cols = slice(unit * 2 * HD, (unit + 1) * 2 * HD)
            first = (offset + part) * group + 2 * pair
            s_mix = jnp.where(tri, raw[0:tokens], raw[2 * tokens :]) + bias_mix
            s_one = raw[tokens : 2 * tokens] + bias_one
            top = jnp.max(jnp.maximum(s_mix, s_one), axis=0, keepdims=True)
            e_mix = jnp.exp2((s_mix - top) * factor)
            e_one = jnp.exp2((s_one - top) * factor)
            inverse = 1.0 / jnp.sum(e_mix + e_one, axis=0, keepdims=True)
            p_mix = e_mix * inverse
            p_one = e_one * inverse
            d_mix = jnp.where(tri, dp[0:tokens], dp[2 * tokens :])
            d_one = dp[tokens : 2 * tokens]
            delta = jnp.sum(p_mix * d_mix + p_one * d_one, axis=0, keepdims=True)
            ds_mix = (p_mix * (d_mix - delta)).astype(jnp.bfloat16)
            ds_one = (p_one * (d_one - delta)).astype(jnp.bfloat16)
            p_mix = p_mix.astype(jnp.bfloat16)
            p_one = p_one.astype(jnp.bfloat16)
            p_ref[:, cols] = p_mix
            ds_ref[0:tokens, cols] = ds_mix
            ds_ref[tokens : 2 * tokens, cols] = ds_one
            sum_k = sum_k + dot(jnp.concatenate([ds_one, ds_mix * far_mask], axis=0), stacked(q_ref, first, 2))
            sum_v = sum_v + dot(jnp.concatenate([p_one, p_mix * far_mask], axis=0), stacked(g_ref, first, 2))
        cols = slice(part * HD, (part + 1) * HD)
        near_ref[0:tokens, cols] = (sum_k[0:tokens] * scale).astype(near_ref.dtype)
        near_ref[tokens : 2 * tokens, cols] = sum_v[0:tokens].astype(near_ref.dtype)
        far_ref[0:tokens, cols] = (sum_k[tokens:] * scale).astype(far_ref.dtype)
        far_ref[tokens : 2 * tokens, cols] = sum_v[tokens:].astype(far_ref.dtype)


def rest_kernel(group, tokens, scale, *refs):
    per = 5
    q_ref, g_ref = refs[0:2]
    chunk_refs = [refs[2 + per * c : 2 + per * (c + 1)] for c in range(CHUNKS)]
    dq_out = refs[2 + per * CHUNKS]
    own_outs = refs[3 + per * CHUNKS : 3 + per * CHUNKS + CHUNKS]
    dq_ref, sems = refs[-2:]
    tri = sees_own(tokens, 2)
    own_mask = jnp.where(tri, 1.0, 0.0).astype(jnp.bfloat16)
    far_mask = jnp.where(tri, 0.0, 1.0).astype(jnp.bfloat16)
    wide = group * HD
    copies = []
    for chunk, (p_ref, ds_ref, own_ref, one_ref, two_ref) in enumerate(chunk_refs):
        count = own_ref.shape[1] // HD
        for part in range(count):
            inner = slice(part * HD, (part + 1) * HD)
            keys_t = jnp.concatenate(
                [jnp.transpose(ref[0:tokens, inner]) for ref in (own_ref, one_ref, two_ref)], axis=1
            )
            sum_k = jnp.zeros((tokens, HD), jnp.float32)
            sum_v = jnp.zeros((tokens, HD), jnp.float32)
            for pair in range(group // 2):
                cols = slice(part * wide + pair * 2 * HD, part * wide + (pair + 1) * 2 * HD)
                first = (chunk * count + part) * group + 2 * pair
                ds_mix = ds_ref[0:tokens, cols]
                ds_own = ds_mix * own_mask
                sum_k = sum_k + dot(ds_own, stacked(q_ref, first, 2))
                sum_v = sum_v + dot(p_ref[:, cols] * own_mask, stacked(g_ref, first, 2))
                rows = jnp.concatenate([ds_own, ds_ref[tokens : 2 * tokens, cols], ds_mix * far_mask], axis=0)
                dq_t = (dot(keys_t, rows) * scale).astype(jnp.bfloat16)
                for h in range(2):
                    dq_ref[:, (first + h) * HD : (first + h + 1) * HD] = jnp.transpose(
                        dq_t[:, h * HD : (h + 1) * HD]
                    )
            own_outs[chunk][0:tokens, inner] = sum_k * scale
            own_outs[chunk][tokens : 2 * tokens, inner] = sum_v
            index = chunk * count + part
            span = pl.ds(index * wide, wide)
            copies.append(pltpu.make_async_copy(dq_ref.at[:, span], dq_out.at[:, span], sems.at[index]))
            copies[-1].start()
    for copy in copies:
        copy.wait()


def final_kernel(tokens, *refs):
    count = (len(refs) - 2) // 3
    k_out, v_out = refs[-2:]
    for index in range(count):
        own_ref, near_ref, far_ref = refs[index : 3 * count : count]
        width = own_ref.shape[1]
        cols = slice(index * width, (index + 1) * width)
        total = own_ref[...] + near_ref[...].astype(jnp.float32) + far_ref[...].astype(jnp.float32)
        k_out[:, cols] = total[0:tokens].astype(k_out.dtype)
        v_out[:, cols] = total[tokens:].astype(v_out.dtype)


def bf16(*shape):
    return jax.ShapeDtypeStruct(shape, jnp.bfloat16)


def f32(*shape):
    return jax.ShapeDtypeStruct(shape, jnp.float32)


def cost(flops, bytes_accessed, transcendentals=0):
    return pl.CostEstimate(flops=flops, bytes_accessed=bytes_accessed, transcendentals=transcendentals)


PARAMS = pltpu.CompilerParams(vmem_limit_bytes=VMEM_LIMIT)


def pack_call(key_states, value_states, segment_ids):
    tokens, width = key_states.shape
    operands = [pltpu.with_memory_space_constraint(x, pltpu.HBM) for x in (key_states, value_states, segment_ids)]
    return pl.pallas_call(
        functools.partial(pack_kernel, tokens),
        in_specs=[pl.BlockSpec(memory_space=pltpu.HBM)] * 3,
        out_shape=[bf16(2 * tokens + (0 if c else SEG_ROWS), width // CHUNKS) for c in range(CHUNKS)],
        scratch_shapes=[
            pltpu.VMEM((tokens,), jnp.int32),
            pltpu.SemaphoreType.DMA((1 + 2 * CHUNKS,)),
        ],
        cost_estimate=cost(0, 8 * tokens * width),
        compiler_params=PARAMS,
        name="pack",
    )(*operands)


def turn_call(q, g):
    tokens, span = q.shape
    operands = [pltpu.with_memory_space_constraint(x, pltpu.HBM) for x in (q, g)]
    return pl.pallas_call(
        turn_kernel,
        in_specs=[pl.BlockSpec(memory_space=pltpu.HBM)] * 2,
        out_shape=[bf16(tokens, span)] * 2 + [bf16(HD, span)] * 2,
        scratch_shapes=[pltpu.SemaphoreType.DMA((2 * HK,))],
        cost_estimate=cost(0, 16 * tokens * span),
        compiler_params=PARAMS,
        name="turn",
    )(*operands)


def score_call(q, g, qt, gt, own, one, two, bias, offset, group, tokens, scale):
    count = own.shape[1] // HD
    span = count * group * HD
    known = bias is not None
    return pl.pallas_call(
        functools.partial(score_kernel, group, tokens, scale, known, offset),
        out_shape=[
            bf16(tokens, span),
            bf16(2 * tokens, span),
            bf16(2 * tokens, count * HD),
            bf16(2 * tokens, count * HD),
        ]
        + [f32(2 * tokens, tokens)] * (not known),
        cost_estimate=cost(2 * tokens * 3 * span * tokens * 4, 12 * tokens * span, 2 * tokens * span),
        compiler_params=PARAMS,
        name="scores",
    )(q, g, qt, gt, own, one, two, *([bias] if known else []))


def rest_call(q, g, parts, group, tokens, scale):
    count = parts[0][2].shape[1] // HD
    return pl.pallas_call(
        functools.partial(rest_kernel, group, tokens, scale),
        out_specs=[pl.BlockSpec(memory_space=pltpu.HBM)] + [pl.BlockSpec(memory_space=pltpu.VMEM)] * CHUNKS,
        out_shape=[bf16(*q.shape)] + [f32(2 * tokens, count * HD)] * CHUNKS,
        scratch_shapes=[pltpu.VMEM(q.shape, jnp.bfloat16), pltpu.SemaphoreType.DMA((HK,))],
        cost_estimate=cost(2 * tokens * 3 * q.shape[1] * tokens * 2, 12 * tokens * q.shape[1]),
        compiler_params=PARAMS,
        name="rest",
    )(q, g, *[x for part in parts for x in part])


def final_call(owns, nears, fars):
    tokens = owns[0].shape[0] // 2
    width = sum(x.shape[1] for x in owns)
    return pl.pallas_call(
        functools.partial(final_kernel, tokens),
        out_shape=[bf16(tokens, width)] * 2,
        cost_estimate=cost(0, 16 * tokens * width),
        compiler_params=PARAMS,
        name="final",
    )(*owns, *nears, *fars)


def shards(queries, key_states, value_states, out_grad, segment_ids):
    tokens = queries.shape[0]
    group = queries.shape[1] // (HK * HD)
    scale = HD ** (-0.5)
    chunks = range(CHUNKS)
    step = HK // CHUNKS
    own = pack_call(key_states, value_states, segment_ids)
    one, two = [], []
    for x in own:
        two.append(shift(x, 2))
        one.append(shift(x, 1))
    q, g, qt, gt = turn_call(queries, out_grad)
    first, near, far, bias = [], [], [], None
    for c in chunks:
        results = score_call(q, g, qt, gt, own[c], one[c], two[c], bias, c * step, group, tokens, scale)
        bias = results[4] if bias is None else bias
        first.append(results)
        far.append(shift(results[2], -2))
        near.append(shift(results[3], -1))
    ds = [x[1] for x in first]
    ds[0], ds[1], near[0], far[0] = lax.optimization_barrier((ds[0], ds[1], near[0], far[0]))
    query_grad, *parts = rest_call(
        q, g, [(first[c][0], ds[c], own[c], one[c], two[c]) for c in chunks], group, tokens, scale
    )
    key_grad, value_grad = final_call(parts, near, far)
    return query_grad, key_grad, value_grad


def solution(mesh):
    rows = P(AXES, None)
    return jax.shard_map(
        shards,
        mesh=mesh,
        in_specs=(rows, rows, rows, rows, P(AXES)),
        out_specs=(rows, rows, rows),
        check_vma=False,
    )
```

```python
import functools

import jax
import jax.numpy as jnp
from jax import lax
from jax.experimental import pallas as pl
from jax.experimental.pallas import tpu as pltpu
from jax.sharding import PartitionSpec as P

HK = 4
HD = 128
SEG_ROWS = 16
NEG = -1e30
LOG2E = 1.4426950408889634
AXES = ("inner", "outer")
CHUNKS = 2
VMEM_LIMIT = 24 * 1024 * 1024


def shift(value, steps):
    count = lax.axis_size(AXES)
    first, last = max(0, -steps), min(count, count - steps)
    return lax.ppermute(value, AXES, [(i, i + steps) for i in range(first, last)])


def dot(a, b):
    return jnp.dot(a, b, preferred_element_type=jnp.float32)


def stacked(ref, first, count):
    return jnp.concatenate(
        [ref[:, (first + h) * HD : (first + h + 1) * HD] for h in range(count)], axis=0
    )


def sees_own(tokens, copies):
    key = lax.broadcasted_iota(jnp.int32, (tokens, tokens), 0)
    query = lax.broadcasted_iota(jnp.int32, (tokens, tokens), 1)
    return jnp.concatenate([key <= query] * copies, axis=1)


def segments(payload, tokens):
    coded = payload[2 * tokens : 2 * tokens + SEG_ROWS, :].astype(jnp.float32)
    row = coded[0:1] * 2.0 + coded[1:2]
    return jnp.broadcast_to(row, (tokens, tokens))


def half_copies(index, tokens, k_ref, v_ref, out_ref, sems):
    width = out_ref.shape[1]
    cols = pl.ds(index * width, width)
    return [
        pltpu.make_async_copy(source.at[:, cols], out_ref.at[pl.ds(half * tokens, tokens), :], sems.at[half])
        for half, source in enumerate((k_ref, v_ref))
    ]


def pack_kernel(tokens, k_ref, v_ref, seg_ref, out_ref, seg_own, sems):
    ids = pltpu.make_async_copy(seg_ref, seg_own, sems.at[2])
    ids.start()
    copies = half_copies(0, tokens, k_ref, v_ref, out_ref, sems)
    for copy in copies:
        copy.start()
    ids.wait()
    seg = jnp.broadcast_to((seg_own[...] + 1)[None, :], (SEG_ROWS, tokens))
    row = lax.broadcasted_iota(jnp.int32, (SEG_ROWS, tokens), 0)
    coded = jnp.where(row == 0, seg >> 1, jnp.where(row == 1, seg & 1, 0))
    coded = coded.astype(jnp.float32).astype(jnp.bfloat16)
    repeats = out_ref.shape[1] // tokens
    out_ref[2 * tokens : 2 * tokens + SEG_ROWS, :] = jnp.concatenate([coded] * repeats, axis=1)
    for copy in copies:
        copy.wait()


def turn_kernel(q_ref, g_ref, k_ref, v_ref, q_out, g_out, qt_ref, gt_ref, kv_out, sems, kv_sems):
    width = q_ref.shape[1] // HK
    halves = half_copies(1, q_ref.shape[0], k_ref, v_ref, kv_out, kv_sems)
    copies = []
    for part in range(HK):
        cols = pl.ds(part * width, width)
        for side, (source, target) in enumerate(((q_ref, q_out), (g_ref, g_out))):
            copies.append(pltpu.make_async_copy(source.at[:, cols], target.at[:, cols], sems.at[2 * part + side]))
    for copy in halves + copies:
        copy.start()
    for part in range(HK):
        for side, (source, target) in enumerate(((q_out, qt_ref), (g_out, gt_ref))):
            copies[2 * part + side].wait()
            for h in range(width // HD):
                cols = slice(part * width + h * HD, part * width + (h + 1) * HD)
                target[:, cols] = jnp.transpose(source[:, cols])
    for copy in halves:
        copy.wait()


def score_kernel(group, tokens, scale, known, offset, q_ref, g_ref, qt_ref, gt_ref, own_ref, one_ref, two_ref,
                 *refs):
    p_ref, ds_ref, far_ref, near_ref = refs[1:] if known else refs[:-1]
    bias_ref = refs[0] if known else refs[-1]
    if known:
        bias = bias_ref[...]
    else:
        ids = slice(0, HD)
        seg_query = segments(own_ref[:, ids], tokens)
        seg_own = jnp.transpose(seg_query)
        seg_one = jnp.transpose(segments(one_ref[:, ids], tokens))
        seg_two = jnp.transpose(segments(two_ref[:, ids], tokens))
        mixed = jnp.where(sees_own(tokens, 1), seg_own, seg_two)
        bias = jnp.concatenate(
            [jnp.where(mixed == seg_query, 0.0, NEG), jnp.where(seg_one == seg_query, 0.0, NEG)], axis=0
        )
        bias_ref[...] = bias
    bias_mix = jnp.concatenate([bias[0:tokens]] * 2, axis=1)
    bias_one = jnp.concatenate([bias[tokens:]] * 2, axis=1)
    tri = sees_own(tokens, 2)
    far_mask = jnp.where(tri, 0.0, 1.0).astype(jnp.bfloat16)
    factor = scale * LOG2E
    pairs = group // 2
    count = own_ref.shape[1] // HD

    def products(unit):
        part, pair = divmod(unit, pairs)
        cols = slice(part * HD, (part + 1) * HD)
        keys, vals = [
            jnp.concatenate([ref[rows, cols] for ref in (own_ref, one_ref, two_ref)], axis=0)
            for rows in (slice(0, tokens), slice(tokens, 2 * tokens))
        ]
        first = (offset + part) * group + 2 * pair
        both = slice(first * HD, (first + 2) * HD)
        return dot(keys, qt_ref[:, both]), dot(vals, gt_ref[:, both])

    ahead = products(0)
    for part in range(count):
        sum_k = jnp.zeros((2 * tokens, HD), jnp.float32)
        sum_v = jnp.zeros((2 * tokens, HD), jnp.float32)
        for pair in range(pairs):
            unit = part * pairs + pair
            raw, dp = ahead
            if unit + 1 < count * pairs:
                ahead = products(unit + 1)
            cols = slice(unit * 2 * HD, (unit + 1) * 2 * HD)
            first = (offset + part) * group + 2 * pair
            s_mix = jnp.where(tri, raw[0:tokens], raw[2 * tokens :]) + bias_mix
            s_one = raw[tokens : 2 * tokens] + bias_one
            top = jnp.max(jnp.maximum(s_mix, s_one), axis=0, keepdims=True)
            e_mix = jnp.exp2((s_mix - top) * factor)
            e_one = jnp.exp2((s_one - top) * factor)
            inverse = 1.0 / jnp.sum(e_mix + e_one, axis=0, keepdims=True)
            p_mix = e_mix * inverse
            p_one = e_one * inverse
            d_mix = jnp.where(tri, dp[0:tokens], dp[2 * tokens :])
            d_one = dp[tokens : 2 * tokens]
            delta = jnp.sum(p_mix * d_mix + p_one * d_one, axis=0, keepdims=True)
            ds_mix = (p_mix * (d_mix - delta)).astype(jnp.bfloat16)
            ds_one = (p_one * (d_one - delta)).astype(jnp.bfloat16)
            p_mix = p_mix.astype(jnp.bfloat16)
            p_one = p_one.astype(jnp.bfloat16)
            p_ref[:, cols] = p_mix
            ds_ref[0:tokens, cols] = ds_mix
            ds_ref[tokens : 2 * tokens, cols] = ds_one
            sum_k = sum_k + dot(jnp.concatenate([ds_one, ds_mix * far_mask], axis=0), stacked(q_ref, first, 2))
            sum_v = sum_v + dot(jnp.concatenate([p_one, p_mix * far_mask], axis=0), stacked(g_ref, first, 2))
        cols = slice(part * HD, (part + 1) * HD)
        near_ref[0:tokens, cols] = (sum_k[0:tokens] * scale).astype(near_ref.dtype)
        near_ref[tokens : 2 * tokens, cols] = sum_v[0:tokens].astype(near_ref.dtype)
        far_ref[0:tokens, cols] = (sum_k[tokens:] * scale).astype(far_ref.dtype)
        far_ref[tokens : 2 * tokens, cols] = sum_v[tokens:].astype(far_ref.dtype)


def rest_kernel(group, tokens, scale, *refs):
    per = 5
    q_ref, g_ref = refs[0:2]
    chunk_refs = [refs[2 + per * c : 2 + per * (c + 1)] for c in range(CHUNKS)]
    dq_out = refs[2 + per * CHUNKS]
    own_outs = refs[3 + per * CHUNKS : 3 + per * CHUNKS + CHUNKS]
    dq_ref, sems = refs[-2:]
    tri = sees_own(tokens, 2)
    own_mask = jnp.where(tri, 1.0, 0.0).astype(jnp.bfloat16)
    far_mask = jnp.where(tri, 0.0, 1.0).astype(jnp.bfloat16)
    wide = group * HD
    copies = []
    for chunk, (p_ref, ds_ref, own_ref, one_ref, two_ref) in enumerate(chunk_refs):
        count = own_ref.shape[1] // HD
        for part in range(count):
            inner = slice(part * HD, (part + 1) * HD)
            keys_t = jnp.concatenate(
                [jnp.transpose(ref[0:tokens, inner]) for ref in (own_ref, one_ref, two_ref)], axis=1
            )
            sum_k = jnp.zeros((tokens, HD), jnp.float32)
            sum_v = jnp.zeros((tokens, HD), jnp.float32)
            for pair in range(group // 2):
                cols = slice(part * wide + pair * 2 * HD, part * wide + (pair + 1) * 2 * HD)
                first = (chunk * count + part) * group + 2 * pair
                ds_mix = ds_ref[0:tokens, cols]
                ds_own = ds_mix * own_mask
                sum_k = sum_k + dot(ds_own, stacked(q_ref, first, 2))
                sum_v = sum_v + dot(p_ref[:, cols] * own_mask, stacked(g_ref, first, 2))
                rows = jnp.concatenate([ds_own, ds_ref[tokens : 2 * tokens, cols], ds_mix * far_mask], axis=0)
                dq_t = (dot(keys_t, rows) * scale).astype(jnp.bfloat16)
                for h in range(2):
                    dq_ref[:, (first + h) * HD : (first + h + 1) * HD] = jnp.transpose(
                        dq_t[:, h * HD : (h + 1) * HD]
                    )
            own_outs[chunk][0:tokens, inner] = sum_k * scale
            own_outs[chunk][tokens : 2 * tokens, inner] = sum_v
            index = chunk * count + part
            span = pl.ds(index * wide, wide)
            copies.append(pltpu.make_async_copy(dq_ref.at[:, span], dq_out.at[:, span], sems.at[index]))
            copies[-1].start()
    for copy in copies:
        copy.wait()


def final_kernel(tokens, *refs):
    count = (len(refs) - 2) // 3
    k_out, v_out = refs[-2:]
    for index in range(count):
        own_ref, near_ref, far_ref = refs[index : 3 * count : count]
        width = own_ref.shape[1]
        cols = slice(index * width, (index + 1) * width)
        total = own_ref[...] + near_ref[...].astype(jnp.float32) + far_ref[...].astype(jnp.float32)
        k_out[:, cols] = total[0:tokens].astype(k_out.dtype)
        v_out[:, cols] = total[tokens:].astype(v_out.dtype)


def bf16(*shape):
    return jax.ShapeDtypeStruct(shape, jnp.bfloat16)


def f32(*shape):
    return jax.ShapeDtypeStruct(shape, jnp.float32)


def cost(flops, bytes_accessed, transcendentals=0):
    return pl.CostEstimate(flops=flops, bytes_accessed=bytes_accessed, transcendentals=transcendentals)


PARAMS = pltpu.CompilerParams(vmem_limit_bytes=VMEM_LIMIT)


def in_hbm(*arrays):
    return [pltpu.with_memory_space_constraint(x, pltpu.HBM) for x in arrays]


def pack_call(key_states, value_states, segment_ids):
    tokens, width = key_states.shape
    return pl.pallas_call(
        functools.partial(pack_kernel, tokens),
        in_specs=[pl.BlockSpec(memory_space=pltpu.HBM)] * 3,
        out_shape=bf16(2 * tokens + SEG_ROWS, width // CHUNKS),
        scratch_shapes=[pltpu.VMEM((tokens,), jnp.int32), pltpu.SemaphoreType.DMA((3,))],
        cost_estimate=cost(0, 4 * tokens * width),
        compiler_params=PARAMS,
        name="pack",
    )(*in_hbm(key_states, value_states, segment_ids))


def turn_call(q, g, key_states, value_states):
    tokens, span = q.shape
    return pl.pallas_call(
        turn_kernel,
        in_specs=[pl.BlockSpec(memory_space=pltpu.HBM)] * 4,
        out_shape=[bf16(tokens, span)] * 2
        + [bf16(HD, span)] * 2
        + [bf16(2 * tokens, key_states.shape[1] // CHUNKS)],
        scratch_shapes=[pltpu.SemaphoreType.DMA((2 * HK,)), pltpu.SemaphoreType.DMA((2,))],
        cost_estimate=cost(0, 16 * tokens * span),
        compiler_params=PARAMS,
        name="turn",
    )(*in_hbm(q, g, key_states, value_states))


def score_call(q, g, qt, gt, own, one, two, bias, offset, group, tokens, scale):
    count = own.shape[1] // HD
    span = count * group * HD
    known = bias is not None
    return pl.pallas_call(
        functools.partial(score_kernel, group, tokens, scale, known, offset),
        out_shape=[
            bf16(tokens, span),
            bf16(2 * tokens, span),
            bf16(2 * tokens, count * HD),
            bf16(2 * tokens, count * HD),
        ]
        + [f32(2 * tokens, tokens)] * (not known),
        cost_estimate=cost(2 * tokens * 3 * span * tokens * 4, 12 * tokens * span, 2 * tokens * span),
        compiler_params=PARAMS,
        name="scores",
    )(q, g, qt, gt, own, one, two, *([bias] if known else []))


def rest_call(q, g, parts, group, tokens, scale):
    count = parts[0][2].shape[1] // HD
    return pl.pallas_call(
        functools.partial(rest_kernel, group, tokens, scale),
        out_specs=[pl.BlockSpec(memory_space=pltpu.HBM)] + [pl.BlockSpec(memory_space=pltpu.VMEM)] * CHUNKS,
        out_shape=[bf16(*q.shape)] + [f32(2 * tokens, count * HD)] * CHUNKS,
        scratch_shapes=[pltpu.VMEM(q.shape, jnp.bfloat16), pltpu.SemaphoreType.DMA((HK,))],
        cost_estimate=cost(2 * tokens * 3 * q.shape[1] * tokens * 2, 12 * tokens * q.shape[1]),
        compiler_params=PARAMS,
        name="rest",
    )(q, g, *[x for part in parts for x in part])


def final_call(owns, nears, fars):
    tokens = owns[0].shape[0] // 2
    width = sum(x.shape[1] for x in owns)
    return pl.pallas_call(
        functools.partial(final_kernel, tokens),
        out_shape=[bf16(tokens, width)] * 2,
        cost_estimate=cost(0, 16 * tokens * width),
        compiler_params=PARAMS,
        name="final",
    )(*owns, *nears, *fars)


def shards(queries, key_states, value_states, out_grad, segment_ids):
    tokens = queries.shape[0]
    group = queries.shape[1] // (HK * HD)
    scale = HD ** (-0.5)
    chunks = range(CHUNKS)
    step = HK // CHUNKS
    own = [pack_call(key_states, value_states, segment_ids)]
    q, g, qt, gt, later = turn_call(queries, out_grad, key_states, value_states)
    own.append(later)
    two = [shift(x, 2) for x in own]
    one = [shift(x, 1) for x in own]
    first, near, far, bias = [], [], [], None
    for c in chunks:
        results = score_call(q, g, qt, gt, own[c], one[c], two[c], bias, c * step, group, tokens, scale)
        bias = results[4] if bias is None else bias
        first.append(results)
        far.append(shift(results[2], -2))
        near.append(shift(results[3], -1))
    ds = [x[1] for x in first]
    ds[0], ds[1], near[0], far[0] = lax.optimization_barrier((ds[0], ds[1], near[0], far[0]))
    query_grad, *parts = rest_call(
        q, g, [(first[c][0], ds[c], own[c], one[c], two[c]) for c in chunks], group, tokens, scale
    )
    key_grad, value_grad = final_call(parts, near, far)
    return query_grad, key_grad, value_grad


def solution(mesh):
    rows = P(AXES, None)
    return jax.shard_map(
        shards,
        mesh=mesh,
        in_specs=(rows, rows, rows, rows, P(AXES)),
        out_specs=(rows, rows, rows),
        check_vma=False,
    )
```

```python
import functools

import jax
import jax.numpy as jnp
from jax import lax
from jax.experimental import pallas as pl
from jax.experimental.pallas import tpu as pltpu
from jax.sharding import PartitionSpec as P

HK = 4
HD = 128
SEG_ROWS = 16
NEG = -1e30
LOG2E = 1.4426950408889634
AXES = ("inner", "outer")
CHUNKS = 2
VMEM_LIMIT = 24 * 1024 * 1024


def shift(value, steps):
    count = lax.axis_size(AXES)
    first, last = max(0, -steps), min(count, count - steps)
    return lax.ppermute(value, AXES, [(i, i + steps) for i in range(first, last)])


def dot(a, b):
    return jnp.dot(a, b, preferred_element_type=jnp.float32)


def stacked(ref, first, count):
    return jnp.concatenate(
        [ref[:, (first + h) * HD : (first + h + 1) * HD] for h in range(count)], axis=0
    )


def sees_own(tokens, copies):
    key = lax.broadcasted_iota(jnp.int32, (tokens, tokens), 0)
    query = lax.broadcasted_iota(jnp.int32, (tokens, tokens), 1)
    return jnp.concatenate([key <= query] * copies, axis=1)


def dot_nt(a, b):
    return lax.dot_general(a, b, (((1,), (1,)), ((), ())), preferred_element_type=jnp.float32)


def segments(ref, first, tokens):
    coded = ref[first : first + SEG_ROWS, :].astype(jnp.float32)
    row = coded[0:1] * 2.0 + coded[1:2]
    return jnp.broadcast_to(row, (tokens, tokens))


def payload_copies(chunk, tokens, k_ref, v_ref, out_ref, sems):
    count = HK // CHUNKS
    return [
        pltpu.make_async_copy(
            source.at[:, pl.ds((chunk * count + part) * HD, HD)],
            out_ref.at[pl.ds((half * count + part) * tokens, tokens), :],
            sems.at[half * count + part],
        )
        for half, source in enumerate((k_ref, v_ref))
        for part in range(count)
    ]


def pack_kernel(tokens, k_ref, v_ref, seg_ref, out_ref, seg_own, sems, seg_sem):
    ids = pltpu.make_async_copy(seg_ref, seg_own, seg_sem.at[0])
    ids.start()
    copies = payload_copies(0, tokens, k_ref, v_ref, out_ref, sems)
    for copy in copies:
        copy.start()
    ids.wait()
    seg = jnp.broadcast_to((seg_own[...] + 1)[None, :], (SEG_ROWS, tokens))
    row = lax.broadcasted_iota(jnp.int32, (SEG_ROWS, tokens), 0)
    coded = jnp.where(row == 0, seg >> 1, jnp.where(row == 1, seg & 1, 0))
    first = out_ref.shape[0] - SEG_ROWS
    out_ref[first : first + SEG_ROWS, :] = coded.astype(jnp.float32).astype(jnp.bfloat16)
    for copy in copies:
        copy.wait()


def turn_kernel(group, q_ref, g_ref, k_ref, v_ref, own_ref, q_out, g_out, qt_ref, gt_ref, kv_out, s_own, d_own,
                sems, kv_sems):
    tokens = q_ref.shape[0]
    width = group * HD
    count = HK // CHUNKS
    halves = payload_copies(1, tokens, k_ref, v_ref, kv_out, kv_sems)
    copies = []
    for part in range(HK):
        cols = pl.ds(part * width, width)
        for side, (source, target) in enumerate(((q_ref, q_out), (g_ref, g_out))):
            copies.append(pltpu.make_async_copy(source.at[:, cols], target.at[:, cols], sems.at[2 * part + side]))
    for copy in halves + copies:
        copy.start()
    for copy in halves:
        copy.wait()
    for part in range(HK):
        payload = (own_ref, kv_out)[part // count]
        for side, (source, target, product) in enumerate(((q_out, qt_ref, s_own), (g_out, gt_ref, d_own))):
            copies[2 * part + side].wait()
            first = (side * count + part % count) * tokens
            block = payload[first : first + tokens, :]
            for pair in range(group // 2):
                cols = slice(part * width + pair * 2 * HD, part * width + (pair + 1) * 2 * HD)
                turned = jnp.concatenate(
                    [jnp.transpose(source[:, cols.start + h * HD : cols.start + (h + 1) * HD]) for h in range(2)],
                    axis=1,
                )
                target[:, cols] = turned
                product[:, cols] = dot(block, turned)


def score_kernel(group, tokens, scale, known, offset, qt_ref, gt_ref, s_own, d_own, own_ref, one_ref, two_ref, *refs):
    p_ref, ds_ref, far_ref, near_ref = refs[1:] if known else refs[:-1]
    bias_ref = refs[0] if known else refs[-1]
    if known:
        bias = bias_ref[...]
    else:
        ids = own_ref.shape[0] - SEG_ROWS
        seg_query = segments(own_ref, ids, tokens)
        seg_own = jnp.transpose(seg_query)
        seg_one = jnp.transpose(segments(one_ref, ids, tokens))
        seg_two = jnp.transpose(segments(two_ref, ids, tokens))
        mixed = jnp.where(sees_own(tokens, 1), seg_own, seg_two)
        bias = jnp.concatenate(
            [jnp.where(mixed == seg_query, 0.0, NEG), jnp.where(seg_one == seg_query, 0.0, NEG)], axis=0
        )
        bias_ref[...] = bias
    bias_mix = jnp.concatenate([bias[0:tokens]] * 2, axis=1)
    bias_one = jnp.concatenate([bias[tokens:]] * 2, axis=1)
    tri = sees_own(tokens, 2)
    far_mask = jnp.where(tri, 0.0, 1.0).astype(jnp.bfloat16)
    factor = scale * LOG2E
    pairs = group // 2
    count = HK // CHUNKS

    def span(unit):
        first = offset * group * HD + unit * 2 * HD
        return slice(first, first + 2 * HD)

    def products(unit):
        part = unit // pairs
        keys, vals = [
            jnp.concatenate([ref[first : first + tokens, :] for ref in (one_ref, two_ref)], axis=0)
            for first in (part * tokens, (count + part) * tokens)
        ]
        return dot(keys, qt_ref[:, span(unit)]), dot(vals, gt_ref[:, span(unit)])

    ahead = products(0)
    for part in range(count):
        sum_k = jnp.zeros((HD, 2 * tokens), jnp.float32)
        sum_v = jnp.zeros((HD, 2 * tokens), jnp.float32)
        for pair in range(pairs):
            unit = part * pairs + pair
            raw, dp = ahead
            if unit + 1 < count * pairs:
                ahead = products(unit + 1)
            cols = slice(unit * 2 * HD, (unit + 1) * 2 * HD)
            s_mix = jnp.where(tri, s_own[:, span(unit)], raw[tokens:]) + bias_mix
            s_one = raw[0:tokens] + bias_one
            top = jnp.max(jnp.maximum(s_mix, s_one), axis=0, keepdims=True)
            e_mix = jnp.exp2((s_mix - top) * factor)
            e_one = jnp.exp2((s_one - top) * factor)
            inverse = 1.0 / jnp.sum(e_mix + e_one, axis=0, keepdims=True)
            p_mix = e_mix * inverse
            p_one = e_one * inverse
            d_mix = jnp.where(tri, d_own[:, span(unit)], dp[tokens:])
            d_one = dp[0:tokens]
            delta = jnp.sum(p_mix * d_mix + p_one * d_one, axis=0, keepdims=True)
            ds_mix = (p_mix * (d_mix - delta)).astype(jnp.bfloat16)
            ds_one = (p_one * (d_one - delta)).astype(jnp.bfloat16)
            p_mix = p_mix.astype(jnp.bfloat16)
            p_one = p_one.astype(jnp.bfloat16)
            p_ref[:, cols] = p_mix
            ds_ref[0:tokens, cols] = ds_mix
            ds_ref[tokens : 2 * tokens, cols] = ds_one
            sum_k = sum_k + dot_nt(qt_ref[:, span(unit)], jnp.concatenate([ds_one, ds_mix * far_mask], axis=0))
            sum_v = sum_v + dot_nt(gt_ref[:, span(unit)], jnp.concatenate([p_one, p_mix * far_mask], axis=0))
        cols = slice(part * HD, (part + 1) * HD)
        for ref, first in ((near_ref, 0), (far_ref, tokens)):
            ref[0:tokens, cols] = jnp.transpose(sum_k[:, first : first + tokens] * scale).astype(ref.dtype)
            ref[tokens : 2 * tokens, cols] = jnp.transpose(sum_v[:, first : first + tokens]).astype(ref.dtype)


def rest_kernel(group, tokens, scale, *refs):
    per = 5
    q_ref, g_ref = refs[0:2]
    chunk_refs = [refs[2 + per * c : 2 + per * (c + 1)] for c in range(CHUNKS)]
    dq_out = refs[2 + per * CHUNKS]
    own_outs = refs[3 + per * CHUNKS : 3 + per * CHUNKS + CHUNKS]
    dq_ref, sems = refs[-2:]
    tri = sees_own(tokens, 2)
    own_mask = jnp.where(tri, 1.0, 0.0).astype(jnp.bfloat16)
    far_mask = jnp.where(tri, 0.0, 1.0).astype(jnp.bfloat16)
    wide = group * HD
    copies = []
    for chunk, (p_ref, ds_ref, own_ref, one_ref, two_ref) in enumerate(chunk_refs):
        count = HK // CHUNKS
        for part in range(count):
            inner = slice(part * HD, (part + 1) * HD)
            block = slice(part * tokens, (part + 1) * tokens)
            keys_t = jnp.concatenate([jnp.transpose(ref[block, :]) for ref in (own_ref, one_ref, two_ref)], axis=1)
            sum_k = jnp.zeros((tokens, HD), jnp.float32)
            sum_v = jnp.zeros((tokens, HD), jnp.float32)
            for pair in range(group // 2):
                cols = slice(part * wide + pair * 2 * HD, part * wide + (pair + 1) * 2 * HD)
                first = (chunk * count + part) * group + 2 * pair
                ds_mix = ds_ref[0:tokens, cols]
                ds_own = ds_mix * own_mask
                sum_k = sum_k + dot(ds_own, stacked(q_ref, first, 2))
                sum_v = sum_v + dot(p_ref[:, cols] * own_mask, stacked(g_ref, first, 2))
                rows = jnp.concatenate([ds_own, ds_ref[tokens : 2 * tokens, cols], ds_mix * far_mask], axis=0)
                dq_t = (dot(keys_t, rows) * scale).astype(jnp.bfloat16)
                for h in range(2):
                    dq_ref[:, (first + h) * HD : (first + h + 1) * HD] = jnp.transpose(
                        dq_t[:, h * HD : (h + 1) * HD]
                    )
            own_outs[chunk][0:tokens, inner] = sum_k * scale
            own_outs[chunk][tokens : 2 * tokens, inner] = sum_v
            index = chunk * count + part
            span = pl.ds(index * wide, wide)
            copies.append(pltpu.make_async_copy(dq_ref.at[:, span], dq_out.at[:, span], sems.at[index]))
            copies[-1].start()
    for copy in copies:
        copy.wait()


def final_kernel(tokens, *refs):
    count = (len(refs) - 2) // 3
    k_out, v_out = refs[-2:]
    for index in range(count):
        own_ref, near_ref, far_ref = refs[index : 3 * count : count]
        width = own_ref.shape[1]
        cols = slice(index * width, (index + 1) * width)
        total = own_ref[...] + near_ref[...].astype(jnp.float32) + far_ref[...].astype(jnp.float32)
        k_out[:, cols] = total[0:tokens].astype(k_out.dtype)
        v_out[:, cols] = total[tokens:].astype(v_out.dtype)


def bf16(*shape):
    return jax.ShapeDtypeStruct(shape, jnp.bfloat16)


def f32(*shape):
    return jax.ShapeDtypeStruct(shape, jnp.float32)


def cost(flops, bytes_accessed, transcendentals=0):
    return pl.CostEstimate(flops=flops, bytes_accessed=bytes_accessed, transcendentals=transcendentals)


PARAMS = pltpu.CompilerParams(vmem_limit_bytes=VMEM_LIMIT)


def in_hbm(*arrays):
    return [pltpu.with_memory_space_constraint(x, pltpu.HBM) for x in arrays]


def pack_call(key_states, value_states, segment_ids):
    tokens, count = key_states.shape[0], HK // CHUNKS
    return pl.pallas_call(
        functools.partial(pack_kernel, tokens),
        in_specs=[pl.BlockSpec(memory_space=pltpu.HBM)] * 3,
        out_shape=bf16(2 * count * tokens + SEG_ROWS, HD),
        scratch_shapes=[
            pltpu.VMEM((tokens,), jnp.int32),
            pltpu.SemaphoreType.DMA((2 * count,)),
            pltpu.SemaphoreType.DMA((1,)),
        ],
        cost_estimate=cost(0, 8 * tokens * count * HD),
        compiler_params=PARAMS,
        name="pack",
    )(*in_hbm(key_states, value_states, segment_ids))


def turn_call(q, g, key_states, value_states, own, group):
    tokens, span = q.shape
    count = HK // CHUNKS
    return pl.pallas_call(
        functools.partial(turn_kernel, group),
        in_specs=[pl.BlockSpec(memory_space=pltpu.HBM)] * 4 + [pl.BlockSpec(memory_space=pltpu.VMEM)],
        out_shape=[bf16(tokens, span)] * 2
        + [bf16(HD, span)] * 2
        + [bf16(2 * count * tokens, HD)]
        + [f32(tokens, span)] * 2,
        scratch_shapes=[pltpu.SemaphoreType.DMA((2 * HK,)), pltpu.SemaphoreType.DMA((2 * count,))],
        cost_estimate=cost(4 * tokens * span * HD, 16 * tokens * span),
        compiler_params=PARAMS,
        name="turn",
    )(*in_hbm(q, g, key_states, value_states), own)


def score_call(qt, gt, s_own, d_own, own, one, two, bias, offset, group, tokens, scale):
    count = HK // CHUNKS
    span = count * group * HD
    known = bias is not None
    return pl.pallas_call(
        functools.partial(score_kernel, group, tokens, scale, known, offset),
        out_shape=[
            bf16(tokens, span),
            bf16(2 * tokens, span),
            bf16(2 * tokens, count * HD),
            bf16(2 * tokens, count * HD),
        ]
        + [f32(2 * tokens, tokens)] * (not known),
        cost_estimate=cost(2 * tokens * 2 * span * tokens * 4, 12 * tokens * span, 2 * tokens * span),
        compiler_params=PARAMS,
        name="scores",
    )(qt, gt, s_own, d_own, own, one, two, *([bias] if known else []))


def rest_call(q, g, parts, group, tokens, scale):
    count = HK // CHUNKS
    return pl.pallas_call(
        functools.partial(rest_kernel, group, tokens, scale),
        out_specs=[pl.BlockSpec(memory_space=pltpu.HBM)] + [pl.BlockSpec(memory_space=pltpu.VMEM)] * CHUNKS,
        out_shape=[bf16(*q.shape)] + [f32(2 * tokens, count * HD)] * CHUNKS,
        scratch_shapes=[pltpu.VMEM(q.shape, jnp.bfloat16), pltpu.SemaphoreType.DMA((HK,))],
        cost_estimate=cost(2 * tokens * 3 * q.shape[1] * tokens * 2, 12 * tokens * q.shape[1]),
        compiler_params=PARAMS,
        name="rest",
    )(q, g, *[x for part in parts for x in part])


def final_call(owns, nears, fars):
    tokens = owns[0].shape[0] // 2
    width = sum(x.shape[1] for x in owns)
    return pl.pallas_call(
        functools.partial(final_kernel, tokens),
        out_shape=[bf16(tokens, width)] * 2,
        cost_estimate=cost(0, 16 * tokens * width),
        compiler_params=PARAMS,
        name="final",
    )(*owns, *nears, *fars)


def shards(queries, key_states, value_states, out_grad, segment_ids):
    tokens = queries.shape[0]
    group = queries.shape[1] // (HK * HD)
    scale = HD ** (-0.5)
    chunks = range(CHUNKS)
    step = HK // CHUNKS
    own = [pack_call(key_states, value_states, segment_ids)]
    q, g, qt, gt, later, s_own, d_own = turn_call(queries, out_grad, key_states, value_states, own[0], group)
    own.append(later)
    one = [shift(x, 1) for x in own]
    two = [shift(x, 2) for x in own]
    first, near, far, bias = [], [], [], None
    for c in chunks:
        results = score_call(qt, gt, s_own, d_own, own[c], one[c], two[c], bias, c * step, group, tokens, scale)
        bias = results[4] if bias is None else bias
        first.append(results)
        far.append(shift(results[2], -2))
        near.append(shift(results[3], -1))
    ds = [x[1] for x in first]
    ds[0], ds[1], near[0], far[0] = lax.optimization_barrier((ds[0], ds[1], near[0], far[0]))
    query_grad, *parts = rest_call(
        q, g, [(first[c][0], ds[c], own[c], one[c], two[c]) for c in chunks], group, tokens, scale
    )
    key_grad, value_grad = final_call(parts, near, far)
    return query_grad, key_grad, value_grad


def solution(mesh):
    rows = P(AXES, None)
    return jax.shard_map(
        shards,
        mesh=mesh,
        in_specs=(rows, rows, rows, rows, P(AXES)),
        out_specs=(rows, rows, rows),
        check_vma=False,
    )
```

```python
import functools

import jax
import jax.numpy as jnp
from jax import lax
from jax.experimental import pallas as pl
from jax.experimental.pallas import tpu as pltpu
from jax.sharding import PartitionSpec as P

HK = 4
HD = 128
SEG_ROWS = 16
NEG = -1e30
LOG2E = 1.4426950408889634
AXES = ("inner", "outer")
CHUNKS = 2
VMEM_LIMIT = 24 * 1024 * 1024


def shift(value, steps):
    count = lax.axis_size(AXES)
    first, last = max(0, -steps), min(count, count - steps)
    return lax.ppermute(value, AXES, [(i, i + steps) for i in range(first, last)])


def dot(a, b):
    return jnp.dot(a, b, preferred_element_type=jnp.float32)


def stacked(ref, first, count):
    return jnp.concatenate(
        [ref[:, (first + h) * HD : (first + h + 1) * HD] for h in range(count)], axis=0
    )


def sees_own(tokens, copies):
    key = lax.broadcasted_iota(jnp.int32, (tokens, tokens), 0)
    query = lax.broadcasted_iota(jnp.int32, (tokens, tokens), 1)
    return jnp.concatenate([key <= query] * copies, axis=1)


def segments(ref, first, tokens):
    coded = ref[first : first + SEG_ROWS, :].astype(jnp.float32)
    row = coded[0:1] * 2.0 + coded[1:2]
    return jnp.broadcast_to(row, (tokens, tokens))


def payload_copies(chunk, tokens, k_ref, v_ref, out_ref, sems):
    count = HK // CHUNKS
    return [
        pltpu.make_async_copy(
            source.at[:, pl.ds((chunk * count + part) * HD, HD)],
            out_ref.at[pl.ds((half * count + part) * tokens, tokens), :],
            sems.at[half * count + part],
        )
        for half, source in enumerate((k_ref, v_ref))
        for part in range(count)
    ]


def pack_kernel(tokens, k_ref, v_ref, seg_ref, out_ref, seg_own, sems, seg_sem):
    ids = pltpu.make_async_copy(seg_ref, seg_own, seg_sem.at[0])
    ids.start()
    copies = payload_copies(0, tokens, k_ref, v_ref, out_ref, sems)
    for copy in copies:
        copy.start()
    ids.wait()
    seg = jnp.broadcast_to((seg_own[...] + 1)[None, :], (SEG_ROWS, tokens))
    row = lax.broadcasted_iota(jnp.int32, (SEG_ROWS, tokens), 0)
    coded = jnp.where(row == 0, seg >> 1, jnp.where(row == 1, seg & 1, 0))
    first = out_ref.shape[0] - SEG_ROWS
    out_ref[first : first + SEG_ROWS, :] = coded.astype(jnp.float32).astype(jnp.bfloat16)
    for copy in copies:
        copy.wait()


def turn_kernel(group, q_ref, g_ref, k_ref, v_ref, q_out, g_out, qt_ref, gt_ref, kv_out, sems, kv_sems):
    width = group * HD
    halves = payload_copies(1, q_ref.shape[0], k_ref, v_ref, kv_out, kv_sems)
    copies = []
    for part in range(HK):
        cols = pl.ds(part * width, width)
        for side, (source, target) in enumerate(((q_ref, q_out), (g_ref, g_out))):
            copies.append(pltpu.make_async_copy(source.at[:, cols], target.at[:, cols], sems.at[2 * part + side]))
    for copy in halves + copies:
        copy.start()
    for part in range(HK):
        for side, (source, target) in enumerate(((q_out, qt_ref), (g_out, gt_ref))):
            copies[2 * part + side].wait()
            for h in range(group):
                cols = slice(part * width + h * HD, part * width + (h + 1) * HD)
                target[:, cols] = jnp.transpose(source[:, cols])
    for copy in halves:
        copy.wait()


def score_kernel(group, tokens, scale, known, offset, q_ref, g_ref, qt_ref, gt_ref, own_ref, one_ref, two_ref, *refs):
    p_ref, ds_ref, far_ref, near_ref = refs[1:] if known else refs[:-1]
    bias_ref = refs[0] if known else refs[-1]
    tri = sees_own(tokens, 1)
    if not known:
        ids = own_ref.shape[0] - SEG_ROWS
        seg_query = segments(own_ref, ids, tokens)
        seg_own = jnp.transpose(seg_query)
        seg_one = jnp.transpose(segments(one_ref, ids, tokens))
        seg_two = jnp.transpose(segments(two_ref, ids, tokens))
        mixed = jnp.where(tri, seg_own, seg_two)
        bias_ref[0:tokens, :] = jnp.where(mixed == seg_query, 0.0, NEG)
        bias_ref[tokens : 2 * tokens, :] = jnp.where(seg_one == seg_query, 0.0, NEG)
    far_mask = jnp.where(tri, 0.0, 1.0).astype(jnp.bfloat16)
    factor = scale * LOG2E
    pairs = group // 2
    count = HK // CHUNKS

    def products(unit):
        part = unit // pairs
        keys, vals = [
            jnp.concatenate([ref[first : first + tokens, :] for ref in (own_ref, one_ref, two_ref)], axis=0)
            for first in (part * tokens, (count + part) * tokens)
        ]
        first = (offset * group + 2 * unit) * HD
        both = slice(first, first + 2 * HD)
        return dot(keys, qt_ref[:, both]), dot(vals, gt_ref[:, both])

    def head(raw, dp, cols):
        s_mix = jnp.where(tri, raw[0:tokens], raw[2 * tokens :]) + bias_ref[0:tokens, :]
        s_one = raw[tokens : 2 * tokens] + bias_ref[tokens : 2 * tokens, :]
        top = jnp.max(jnp.maximum(s_mix, s_one), axis=0, keepdims=True)
        e_mix = jnp.exp2((s_mix - top) * factor)
        e_one = jnp.exp2((s_one - top) * factor)
        inverse = 1.0 / jnp.sum(e_mix + e_one, axis=0, keepdims=True)
        p_mix = e_mix * inverse
        p_one = e_one * inverse
        d_mix = jnp.where(tri, dp[0:tokens], dp[2 * tokens :])
        d_one = dp[tokens : 2 * tokens]
        delta = jnp.sum(p_mix * d_mix + p_one * d_one, axis=0, keepdims=True)
        ds_mix = (p_mix * (d_mix - delta)).astype(jnp.bfloat16)
        ds_one = (p_one * (d_one - delta)).astype(jnp.bfloat16)
        p_mix = p_mix.astype(jnp.bfloat16)
        p_one = p_one.astype(jnp.bfloat16)
        p_ref[:, cols] = p_mix
        ds_ref[0:tokens, cols] = ds_mix
        ds_ref[tokens : 2 * tokens, cols] = ds_one
        return (
            jnp.concatenate([p_one, p_mix * far_mask], axis=0),
            jnp.concatenate([ds_one, ds_mix * far_mask], axis=0),
        )

    ahead = products(0)
    for part in range(count):
        probs, grads = [], []
        for pair in range(pairs):
            unit = part * pairs + pair
            raw, dp = ahead
            if unit + 1 < count * pairs:
                ahead = products(unit + 1)
            for h in range(2):
                inner = slice(h * HD, (h + 1) * HD)
                p, ds = head(raw[:, inner], dp[:, inner], slice((2 * unit + h) * HD, (2 * unit + h + 1) * HD))
                probs.append(p)
                grads.append(ds)
        first = (offset + part) * group
        sum_k = dot(jnp.concatenate(grads, axis=1), stacked(q_ref, first, group)) * scale
        sum_v = dot(jnp.concatenate(probs, axis=1), stacked(g_ref, first, group))
        cols = slice(part * HD, (part + 1) * HD)
        for ref, row in ((near_ref, 0), (far_ref, tokens)):
            ref[0:tokens, cols] = sum_k[row : row + tokens].astype(ref.dtype)
            ref[tokens : 2 * tokens, cols] = sum_v[row : row + tokens].astype(ref.dtype)


def rest_kernel(group, tokens, scale, *refs):
    per = 5
    q_ref, g_ref = refs[0:2]
    chunk_refs = [refs[2 + per * c : 2 + per * (c + 1)] for c in range(CHUNKS)]
    dq_out = refs[2 + per * CHUNKS]
    own_outs = refs[3 + per * CHUNKS : 3 + per * CHUNKS + CHUNKS]
    dq_ref, sems = refs[-2:]
    tri = sees_own(tokens, 2)
    own_mask = jnp.where(tri, 1.0, 0.0).astype(jnp.bfloat16)
    far_mask = jnp.where(tri, 0.0, 1.0).astype(jnp.bfloat16)
    wide = group * HD
    copies = []
    for chunk, (p_ref, ds_ref, own_ref, one_ref, two_ref) in enumerate(chunk_refs):
        count = HK // CHUNKS
        for part in range(count):
            inner = slice(part * HD, (part + 1) * HD)
            block = slice(part * tokens, (part + 1) * tokens)
            keys_t = jnp.concatenate([jnp.transpose(ref[block, :]) for ref in (own_ref, one_ref, two_ref)], axis=1)
            sum_k = jnp.zeros((tokens, HD), jnp.float32)
            sum_v = jnp.zeros((tokens, HD), jnp.float32)
            for pair in range(group // 2):
                cols = slice(part * wide + pair * 2 * HD, part * wide + (pair + 1) * 2 * HD)
                first = (chunk * count + part) * group + 2 * pair
                ds_mix = ds_ref[0:tokens, cols]
                ds_own = ds_mix * own_mask
                sum_k = sum_k + dot(ds_own, stacked(q_ref, first, 2))
                sum_v = sum_v + dot(p_ref[:, cols] * own_mask, stacked(g_ref, first, 2))
                rows = jnp.concatenate([ds_own, ds_ref[tokens : 2 * tokens, cols], ds_mix * far_mask], axis=0)
                dq_t = (dot(keys_t, rows) * scale).astype(jnp.bfloat16)
                for h in range(2):
                    dq_ref[:, (first + h) * HD : (first + h + 1) * HD] = jnp.transpose(
                        dq_t[:, h * HD : (h + 1) * HD]
                    )
            own_outs[chunk][0:tokens, inner] = sum_k * scale
            own_outs[chunk][tokens : 2 * tokens, inner] = sum_v
            index = chunk * count + part
            span = pl.ds(index * wide, wide)
            copies.append(pltpu.make_async_copy(dq_ref.at[:, span], dq_out.at[:, span], sems.at[index]))
            copies[-1].start()
    for copy in copies:
        copy.wait()


def final_kernel(tokens, *refs):
    count = (len(refs) - 2) // 3
    k_out, v_out = refs[-2:]
    for index in range(count):
        own_ref, near_ref, far_ref = refs[index : 3 * count : count]
        width = own_ref.shape[1]
        cols = slice(index * width, (index + 1) * width)
        total = own_ref[...] + near_ref[...].astype(jnp.float32) + far_ref[...].astype(jnp.float32)
        k_out[:, cols] = total[0:tokens].astype(k_out.dtype)
        v_out[:, cols] = total[tokens:].astype(v_out.dtype)


def bf16(*shape):
    return jax.ShapeDtypeStruct(shape, jnp.bfloat16)


def f32(*shape):
    return jax.ShapeDtypeStruct(shape, jnp.float32)


def cost(flops, bytes_accessed, transcendentals=0):
    return pl.CostEstimate(flops=flops, bytes_accessed=bytes_accessed, transcendentals=transcendentals)


PARAMS = pltpu.CompilerParams(vmem_limit_bytes=VMEM_LIMIT)


def in_hbm(*arrays):
    return [pltpu.with_memory_space_constraint(x, pltpu.HBM) for x in arrays]


def pack_call(key_states, value_states, segment_ids):
    tokens, count = key_states.shape[0], HK // CHUNKS
    return pl.pallas_call(
        functools.partial(pack_kernel, tokens),
        in_specs=[pl.BlockSpec(memory_space=pltpu.HBM)] * 3,
        out_shape=bf16(2 * count * tokens + SEG_ROWS, HD),
        scratch_shapes=[
            pltpu.VMEM((tokens,), jnp.int32),
            pltpu.SemaphoreType.DMA((2 * count,)),
            pltpu.SemaphoreType.DMA((1,)),
        ],
        cost_estimate=cost(0, 8 * tokens * count * HD),
        compiler_params=PARAMS,
        name="pack",
    )(*in_hbm(key_states, value_states, segment_ids))


def turn_call(q, g, key_states, value_states, group):
    tokens, span = q.shape
    count = HK // CHUNKS
    return pl.pallas_call(
        functools.partial(turn_kernel, group),
        in_specs=[pl.BlockSpec(memory_space=pltpu.HBM)] * 4,
        out_shape=[bf16(tokens, span)] * 2 + [bf16(HD, span)] * 2 + [bf16(2 * count * tokens, HD)],
        scratch_shapes=[pltpu.SemaphoreType.DMA((2 * HK,)), pltpu.SemaphoreType.DMA((2 * count,))],
        cost_estimate=cost(0, 16 * tokens * span),
        compiler_params=PARAMS,
        name="turn",
    )(*in_hbm(q, g, key_states, value_states))


def score_call(q, g, qt, gt, own, one, two, bias, offset, group, tokens, scale):
    count = HK // CHUNKS
    span = count * group * HD
    known = bias is not None
    return pl.pallas_call(
        functools.partial(score_kernel, group, tokens, scale, known, offset),
        out_shape=[
            bf16(tokens, span),
            bf16(2 * tokens, span),
            bf16(2 * tokens, count * HD),
            bf16(2 * tokens, count * HD),
        ]
        + [f32(2 * tokens, tokens)] * (not known),
        cost_estimate=cost(2 * tokens * 3 * span * tokens * 4, 12 * tokens * span, 2 * tokens * span),
        compiler_params=PARAMS,
        name="scores",
    )(q, g, qt, gt, own, one, two, *([bias] if known else []))


def rest_call(q, g, parts, group, tokens, scale):
    count = HK // CHUNKS
    return pl.pallas_call(
        functools.partial(rest_kernel, group, tokens, scale),
        out_specs=[pl.BlockSpec(memory_space=pltpu.HBM)] + [pl.BlockSpec(memory_space=pltpu.VMEM)] * CHUNKS,
        out_shape=[bf16(*q.shape)] + [f32(2 * tokens, count * HD)] * CHUNKS,
        scratch_shapes=[pltpu.VMEM(q.shape, jnp.bfloat16), pltpu.SemaphoreType.DMA((HK,))],
        cost_estimate=cost(2 * tokens * 3 * q.shape[1] * tokens * 2, 12 * tokens * q.shape[1]),
        compiler_params=PARAMS,
        name="rest",
    )(q, g, *[x for part in parts for x in part])


def final_call(owns, nears, fars):
    tokens = owns[0].shape[0] // 2
    width = sum(x.shape[1] for x in owns)
    return pl.pallas_call(
        functools.partial(final_kernel, tokens),
        out_shape=[bf16(tokens, width)] * 2,
        cost_estimate=cost(0, 16 * tokens * width),
        compiler_params=PARAMS,
        name="final",
    )(*owns, *nears, *fars)


def shards(queries, key_states, value_states, out_grad, segment_ids):
    tokens = queries.shape[0]
    group = queries.shape[1] // (HK * HD)
    scale = HD ** (-0.5)
    chunks = range(CHUNKS)
    step = HK // CHUNKS
    own = [pack_call(key_states, value_states, segment_ids)]
    q, g, qt, gt, later = turn_call(queries, out_grad, key_states, value_states, group)
    own.append(later)
    one = [shift(x, 1) for x in own]
    two = [shift(x, 2) for x in own]
    first, near, far, bias = [], [], [], None
    for c in chunks:
        results = score_call(q, g, qt, gt, own[c], one[c], two[c], bias, c * step, group, tokens, scale)
        bias = results[4] if bias is None else bias
        first.append(results)
        far.append(shift(results[2], -2))
        near.append(shift(results[3], -1))
    ds = [x[1] for x in first]
    ds[0], ds[1], near[0], far[0] = lax.optimization_barrier((ds[0], ds[1], near[0], far[0]))
    query_grad, *parts = rest_call(
        q, g, [(first[c][0], ds[c], own[c], one[c], two[c]) for c in chunks], group, tokens, scale
    )
    key_grad, value_grad = final_call(parts, near, far)
    return query_grad, key_grad, value_grad


def solution(mesh):
    rows = P(AXES, None)
    return jax.shard_map(
        shards,
        mesh=mesh,
        in_specs=(rows, rows, rows, rows, P(AXES)),
        out_specs=(rows, rows, rows),
        check_vma=False,
    )
```

```python
import functools

import jax
import jax.numpy as jnp
from jax import lax
from jax.experimental import pallas as pl
from jax.experimental.pallas import tpu as pltpu
from jax.sharding import PartitionSpec as P

HK = 4
HD = 128
SEG_ROWS = 16
NEG = -1e30
LOG2E = 1.4426950408889634
AXES = ("inner", "outer")
CHUNKS = 2
UNIT = 4
VMEM_LIMIT = 24 * 1024 * 1024


def shift(value, steps):
    count = lax.axis_size(AXES)
    first, last = max(0, -steps), min(count, count - steps)
    return lax.ppermute(value, AXES, [(i, i + steps) for i in range(first, last)])


def dot(a, b):
    return jnp.dot(a, b, preferred_element_type=jnp.float32)


def stacked(ref, first, count):
    return jnp.concatenate(
        [ref[:, (first + h) * HD : (first + h + 1) * HD] for h in range(count)], axis=0
    )


def sees_own(tokens, copies):
    key = lax.broadcasted_iota(jnp.int32, (tokens, tokens), 0)
    query = lax.broadcasted_iota(jnp.int32, (tokens, tokens), 1)
    return jnp.concatenate([key <= query] * copies, axis=1)


def segments(ref, first, tokens):
    coded = ref[first : first + SEG_ROWS, :].astype(jnp.float32)
    row = coded[0:1] * 2.0 + coded[1:2]
    return jnp.broadcast_to(row, (tokens, tokens))


def payload_copies(chunk, tokens, k_ref, v_ref, out_ref, sems):
    count = HK // CHUNKS
    return [
        pltpu.make_async_copy(
            source.at[:, pl.ds((chunk * count + part) * HD, HD)],
            out_ref.at[pl.ds((half * count + part) * tokens, tokens), :],
            sems.at[half * count + part],
        )
        for half, source in enumerate((k_ref, v_ref))
        for part in range(count)
    ]


def pack_kernel(tokens, k_ref, v_ref, seg_ref, out_ref, seg_own, sems, seg_sem):
    ids = pltpu.make_async_copy(seg_ref, seg_own, seg_sem.at[0])
    ids.start()
    copies = payload_copies(0, tokens, k_ref, v_ref, out_ref, sems)
    for copy in copies:
        copy.start()
    ids.wait()
    seg = jnp.broadcast_to((seg_own[...] + 1)[None, :], (SEG_ROWS, tokens))
    row = lax.broadcasted_iota(jnp.int32, (SEG_ROWS, tokens), 0)
    coded = jnp.where(row == 0, seg >> 1, jnp.where(row == 1, seg & 1, 0))
    first = out_ref.shape[0] - SEG_ROWS
    out_ref[first : first + SEG_ROWS, :] = coded.astype(jnp.float32).astype(jnp.bfloat16)
    for copy in copies:
        copy.wait()


def turn_kernel(group, q_ref, g_ref, k_ref, v_ref, q_out, g_out, qt_ref, gt_ref, kv_out, sems, kv_sems):
    width = group * HD
    halves = payload_copies(1, q_ref.shape[0], k_ref, v_ref, kv_out, kv_sems)
    copies = []
    for part in range(HK):
        cols = pl.ds(part * width, width)
        for side, (source, target) in enumerate(((q_ref, q_out), (g_ref, g_out))):
            copies.append(pltpu.make_async_copy(source.at[:, cols], target.at[:, cols], sems.at[2 * part + side]))
    for copy in halves + copies:
        copy.start()
    for part in range(HK):
        for side, (source, target) in enumerate(((q_out, qt_ref), (g_out, gt_ref))):
            copies[2 * part + side].wait()
            for h in range(group):
                cols = slice(part * width + h * HD, part * width + (h + 1) * HD)
                target[:, cols] = jnp.transpose(source[:, cols])
    for copy in halves:
        copy.wait()


def score_kernel(group, tokens, scale, known, offset, q_ref, g_ref, qt_ref, gt_ref, own_ref, two_ref, one_ref, *refs):
    p_ref, ds_ref, far_ref, near_ref = refs[1:] if known else refs[:-1]
    bias_ref = refs[0] if known else refs[-1]
    tri = sees_own(tokens, 1)
    if not known:
        ids = own_ref.shape[0] - SEG_ROWS
        seg_query = segments(own_ref, ids, tokens)
        seg_own = jnp.transpose(seg_query)
        seg_one = jnp.transpose(segments(one_ref, ids, tokens))
        seg_two = jnp.transpose(segments(two_ref, ids, tokens))
        mixed = jnp.where(tri, seg_own, seg_two)
        bias_ref[0:tokens, :] = jnp.where(mixed == seg_query, 0.0, NEG)
        bias_ref[tokens : 2 * tokens, :] = jnp.where(seg_one == seg_query, 0.0, NEG)
    wide = UNIT * HD
    tri = sees_own(tokens, UNIT)
    far_mask = jnp.where(tri, 0.0, 1.0).astype(jnp.bfloat16)
    bias_mix = jnp.concatenate([bias_ref[0:tokens, :]] * UNIT, axis=1)
    bias_one = jnp.concatenate([bias_ref[tokens : 2 * tokens, :]] * UNIT, axis=1)
    factor = scale * LOG2E
    units = group // UNIT
    count = HK // CHUNKS

    def products(unit):
        part = unit // units
        keys, vals = [
            jnp.concatenate([ref[first : first + tokens, :] for ref in (own_ref, one_ref, two_ref)], axis=0)
            for first in (part * tokens, (count + part) * tokens)
        ]
        first = offset * group * HD + unit * wide
        return dot(keys, qt_ref[:, first : first + wide]), dot(vals, gt_ref[:, first : first + wide])

    ahead = products(0)
    for part in range(count):
        sum_k = jnp.zeros((2 * tokens, HD), jnp.float32)
        sum_v = jnp.zeros((2 * tokens, HD), jnp.float32)
        for step in range(units):
            unit = part * units + step
            raw, dp = ahead
            if unit + 1 < count * units:
                ahead = products(unit + 1)
            cols = slice(unit * wide, (unit + 1) * wide)
            s_mix = jnp.where(tri, raw[0:tokens], raw[2 * tokens :]) + bias_mix
            s_one = raw[tokens : 2 * tokens] + bias_one
            top = jnp.max(jnp.maximum(s_mix, s_one), axis=0, keepdims=True)
            e_mix = jnp.exp2((s_mix - top) * factor)
            e_one = jnp.exp2((s_one - top) * factor)
            inverse = 1.0 / jnp.sum(e_mix + e_one, axis=0, keepdims=True)
            p_mix = e_mix * inverse
            p_one = e_one * inverse
            d_mix = jnp.where(tri, dp[0:tokens], dp[2 * tokens :])
            d_one = dp[tokens : 2 * tokens]
            delta = jnp.sum(p_mix * d_mix + p_one * d_one, axis=0, keepdims=True)
            ds_mix = (p_mix * (d_mix - delta)).astype(jnp.bfloat16)
            ds_one = (p_one * (d_one - delta)).astype(jnp.bfloat16)
            p_mix = p_mix.astype(jnp.bfloat16)
            p_one = p_one.astype(jnp.bfloat16)
            p_ref[:, cols] = p_mix
            ds_ref[0:tokens, cols] = ds_mix
            ds_ref[tokens : 2 * tokens, cols] = ds_one
            first = offset * group + unit * UNIT
            sum_k = sum_k + dot(jnp.concatenate([ds_one, ds_mix * far_mask], axis=0), stacked(q_ref, first, UNIT))
            sum_v = sum_v + dot(jnp.concatenate([p_one, p_mix * far_mask], axis=0), stacked(g_ref, first, UNIT))
        sum_k = sum_k * scale
        cols = slice(part * HD, (part + 1) * HD)
        for ref, row in ((near_ref, 0), (far_ref, tokens)):
            ref[0:tokens, cols] = sum_k[row : row + tokens].astype(ref.dtype)
            ref[tokens : 2 * tokens, cols] = sum_v[row : row + tokens].astype(ref.dtype)


def leave(total, index, tokens, kv_ref, k_out, v_out, sems):
    width = total.shape[1]
    kv_ref[...] = total.astype(kv_ref.dtype)
    copies = [
        pltpu.make_async_copy(
            kv_ref.at[pl.ds(half * tokens, tokens), :], out.at[:, pl.ds(index * width, width)], sems.at[half]
        )
        for half, out in enumerate((k_out, v_out))
    ]
    for copy in copies:
        copy.start()
    return copies


def rest_kernel(group, tokens, scale, q_ref, g_ref, far_ref, near_ref, *refs):
    per = 5
    chunk_refs = [refs[per * c : per * (c + 1)] for c in range(CHUNKS)]
    dq_out, k_out, v_out, own_out, dq_ref, kv_ref, sems, kv_sems = refs[per * CHUNKS :]
    tri = sees_own(tokens, 2)
    own_mask = jnp.where(tri, 1.0, 0.0).astype(jnp.bfloat16)
    far_mask = jnp.where(tri, 0.0, 1.0).astype(jnp.bfloat16)
    wide = group * HD
    count = HK // CHUNKS
    copies = []
    for chunk, (p_ref, ds_ref, own_ref, two_ref, one_ref) in enumerate(chunk_refs):
        sums = []
        for part in range(count):
            block = slice(part * tokens, (part + 1) * tokens)
            keys_t = jnp.concatenate([jnp.transpose(ref[block, :]) for ref in (own_ref, one_ref, two_ref)], axis=1)
            sum_k = jnp.zeros((tokens, HD), jnp.float32)
            sum_v = jnp.zeros((tokens, HD), jnp.float32)
            for pair in range(group // 2):
                cols = slice(part * wide + pair * 2 * HD, part * wide + (pair + 1) * 2 * HD)
                first = (chunk * count + part) * group + 2 * pair
                ds_mix = ds_ref[0:tokens, cols]
                ds_own = ds_mix * own_mask
                sum_k = sum_k + dot(ds_own, stacked(q_ref, first, 2))
                sum_v = sum_v + dot(p_ref[:, cols] * own_mask, stacked(g_ref, first, 2))
                rows = jnp.concatenate([ds_own, ds_ref[tokens : 2 * tokens, cols], ds_mix * far_mask], axis=0)
                dq_t = (dot(keys_t, rows) * scale).astype(jnp.bfloat16)
                for h in range(2):
                    dq_ref[:, (first + h) * HD : (first + h + 1) * HD] = jnp.transpose(
                        dq_t[:, h * HD : (h + 1) * HD]
                    )
            sums.append(jnp.concatenate([sum_k * scale, sum_v], axis=0))
            index = chunk * count + part
            span = pl.ds(index * wide, wide)
            copies.append(pltpu.make_async_copy(dq_ref.at[:, span], dq_out.at[:, span], sems.at[index]))
            copies[-1].start()
        total = jnp.concatenate(sums, axis=1)
        if chunk == 0:
            total = total + near_ref[...].astype(jnp.float32) + far_ref[...].astype(jnp.float32)
            copies += leave(total, 0, tokens, kv_ref, k_out, v_out, kv_sems)
        else:
            own_out[...] = total
    for copy in copies:
        copy.wait()


def final_kernel(tokens, own_ref, far_ref, near_ref, k_before, v_before, k_out, v_out, kv_ref, sems):
    total = own_ref[...] + near_ref[...].astype(jnp.float32) + far_ref[...].astype(jnp.float32)
    for copy in leave(total, 1, tokens, kv_ref, k_out, v_out, sems):
        copy.wait()


def bf16(*shape):
    return jax.ShapeDtypeStruct(shape, jnp.bfloat16)


def f32(*shape):
    return jax.ShapeDtypeStruct(shape, jnp.float32)


def cost(flops, bytes_accessed, transcendentals=0):
    return pl.CostEstimate(flops=flops, bytes_accessed=bytes_accessed, transcendentals=transcendentals)


PARAMS = pltpu.CompilerParams(vmem_limit_bytes=VMEM_LIMIT)


def in_hbm(*arrays):
    return [pltpu.with_memory_space_constraint(x, pltpu.HBM) for x in arrays]


def pack_call(key_states, value_states, segment_ids):
    tokens, count = key_states.shape[0], HK // CHUNKS
    return pl.pallas_call(
        functools.partial(pack_kernel, tokens),
        in_specs=[pl.BlockSpec(memory_space=pltpu.HBM)] * 3,
        out_shape=bf16(2 * count * tokens + SEG_ROWS, HD),
        scratch_shapes=[
            pltpu.VMEM((tokens,), jnp.int32),
            pltpu.SemaphoreType.DMA((2 * count,)),
            pltpu.SemaphoreType.DMA((1,)),
        ],
        cost_estimate=cost(0, 8 * tokens * count * HD),
        compiler_params=PARAMS,
        name="pack",
    )(*in_hbm(key_states, value_states, segment_ids))


def turn_call(q, g, key_states, value_states, group):
    tokens, span = q.shape
    count = HK // CHUNKS
    return pl.pallas_call(
        functools.partial(turn_kernel, group),
        in_specs=[pl.BlockSpec(memory_space=pltpu.HBM)] * 4,
        out_shape=[bf16(tokens, span)] * 2 + [bf16(HD, span)] * 2 + [bf16(2 * count * tokens, HD)],
        scratch_shapes=[pltpu.SemaphoreType.DMA((2 * HK,)), pltpu.SemaphoreType.DMA((2 * count,))],
        cost_estimate=cost(0, 16 * tokens * span),
        compiler_params=PARAMS,
        name="turn",
    )(*in_hbm(q, g, key_states, value_states))


def score_call(q, g, qt, gt, own, two, one, bias, offset, group, tokens, scale):
    count = HK // CHUNKS
    span = count * group * HD
    known = bias is not None
    return pl.pallas_call(
        functools.partial(score_kernel, group, tokens, scale, known, offset),
        out_shape=[
            bf16(tokens, span),
            bf16(2 * tokens, span),
            bf16(2 * tokens, count * HD),
            bf16(2 * tokens, count * HD),
        ]
        + [f32(2 * tokens, tokens)] * (not known),
        cost_estimate=cost(2 * tokens * 3 * span * tokens * 4, 12 * tokens * span, 2 * tokens * span),
        compiler_params=PARAMS,
        name="scores",
    )(q, g, qt, gt, own, two, one, *([bias] if known else []))


ON_CHIP = pl.BlockSpec(memory_space=pltpu.VMEM)
IN_HBM = pl.BlockSpec(memory_space=pltpu.HBM)


def rest_call(q, g, far, near, parts, group, tokens, scale):
    grads = bf16(tokens, HK * HD)
    chunk = (2 * tokens, HK // CHUNKS * HD)
    return pl.pallas_call(
        functools.partial(rest_kernel, group, tokens, scale),
        out_specs=[IN_HBM] * 3 + [ON_CHIP],
        out_shape=[bf16(*q.shape), grads, grads, f32(*chunk)],
        scratch_shapes=[
            pltpu.VMEM(q.shape, jnp.bfloat16),
            pltpu.VMEM(chunk, jnp.bfloat16),
            pltpu.SemaphoreType.DMA((HK,)),
            pltpu.SemaphoreType.DMA((2,)),
        ],
        cost_estimate=cost(2 * tokens * 3 * q.shape[1] * tokens * 2, 12 * tokens * q.shape[1]),
        compiler_params=PARAMS,
        name="rest",
    )(q, g, far, near, *[x for part in parts for x in part])


def final_call(own, far, near, key_grad, value_grad):
    return pl.pallas_call(
        functools.partial(final_kernel, key_grad.shape[0]),
        in_specs=[ON_CHIP] * 3 + [IN_HBM] * 2,
        out_specs=[IN_HBM] * 2,
        out_shape=[bf16(*key_grad.shape)] * 2,
        scratch_shapes=[pltpu.VMEM(own.shape, jnp.bfloat16), pltpu.SemaphoreType.DMA((2,))],
        input_output_aliases={3: 0, 4: 1},
        cost_estimate=cost(0, 16 * own.shape[0] * own.shape[1]),
        compiler_params=PARAMS,
        name="final",
    )(own, far, near, key_grad, value_grad)


def shards(queries, key_states, value_states, out_grad, segment_ids):
    tokens = queries.shape[0]
    group = queries.shape[1] // (HK * HD)
    scale = HD ** (-0.5)
    chunks = range(CHUNKS)
    step = HK // CHUNKS
    own = [pack_call(key_states, value_states, segment_ids)]
    q, g, qt, gt, later = turn_call(queries, out_grad, key_states, value_states, group)
    own.append(later)
    two = [shift(x, 2) for x in own]
    one = [shift(x, 1) for x in own]
    first, near, far, bias = [], [], [], None
    for c in chunks:
        results = score_call(q, g, qt, gt, own[c], two[c], one[c], bias, c * step, group, tokens, scale)
        bias = results[4] if bias is None else bias
        first.append(results)
        far.append(shift(results[2], -2))
        near.append(shift(results[3], -1))
    query_grad, key_grad, value_grad, own_terms = rest_call(
        q, g, far[0], near[0], [(first[c][0], first[c][1], own[c], two[c], one[c]) for c in chunks],
        group, tokens, scale,
    )
    key_grad, value_grad = final_call(own_terms, far[1], near[1], key_grad, value_grad)
    return query_grad, key_grad, value_grad


def solution(mesh):
    rows = P(AXES, None)
    return jax.shard_map(
        shards,
        mesh=mesh,
        in_specs=(rows, rows, rows, rows, P(AXES)),
        out_specs=(rows, rows, rows),
        check_vma=False,
    )
```

```python
import functools

import jax
import jax.numpy as jnp
from jax import lax
from jax.experimental import pallas as pl
from jax.experimental.pallas import tpu as pltpu
from jax.sharding import PartitionSpec as P

HK = 4
HD = 128
SEG_ROWS = 16
NEG = -1e30
LOG2E = 1.4426950408889634
AXES = ("inner", "outer")
CHUNKS = 2
UNIT = 4
VMEM_LIMIT = 24 * 1024 * 1024


def shift(value, steps):
    count = lax.axis_size(AXES)
    first, last = max(0, -steps), min(count, count - steps)
    return lax.ppermute(value, AXES, [(i, i + steps) for i in range(first, last)])


def dot(a, b):
    return jnp.dot(a, b, preferred_element_type=jnp.float32)


def stacked(ref, first, count):
    return jnp.concatenate(
        [ref[:, (first + h) * HD : (first + h + 1) * HD] for h in range(count)], axis=0
    )


def sees_own(tokens, copies):
    key = lax.broadcasted_iota(jnp.int32, (tokens, tokens), 0)
    query = lax.broadcasted_iota(jnp.int32, (tokens, tokens), 1)
    return jnp.concatenate([key <= query] * copies, axis=1)


def segments(ref, first, tokens):
    coded = ref[first : first + SEG_ROWS, :].astype(jnp.float32)
    row = coded[0:1] * 2.0 + coded[1:2]
    return jnp.broadcast_to(row, (tokens, tokens))


def payload_copies(chunk, tokens, k_ref, v_ref, out_ref, sems):
    count = HK // CHUNKS
    return [
        pltpu.make_async_copy(
            source.at[:, pl.ds((chunk * count + part) * HD, HD)],
            out_ref.at[pl.ds((half * count + part) * tokens, tokens), :],
            sems.at[half * count + part],
        )
        for half, source in enumerate((k_ref, v_ref))
        for part in range(count)
    ]


def pack_kernel(tokens, k_ref, v_ref, seg_ref, out_ref, seg_own, sems, seg_sem):
    ids = pltpu.make_async_copy(seg_ref, seg_own, seg_sem.at[0])
    ids.start()
    copies = payload_copies(0, tokens, k_ref, v_ref, out_ref, sems)
    for copy in copies:
        copy.start()
    ids.wait()
    seg = jnp.broadcast_to((seg_own[...] + 1)[None, :], (SEG_ROWS, tokens))
    row = lax.broadcasted_iota(jnp.int32, (SEG_ROWS, tokens), 0)
    coded = jnp.where(row == 0, seg >> 1, jnp.where(row == 1, seg & 1, 0))
    first = out_ref.shape[0] - SEG_ROWS
    out_ref[first : first + SEG_ROWS, :] = coded.astype(jnp.float32).astype(jnp.bfloat16)
    for copy in copies:
        copy.wait()


def turn_kernel(group, q_ref, g_ref, k_ref, v_ref, q_out, g_out, qt_ref, gt_ref, kv_out, sems, kv_sems):
    width = group * HD
    halves = payload_copies(1, q_ref.shape[0], k_ref, v_ref, kv_out, kv_sems)
    copies = []
    for part in range(HK):
        cols = pl.ds(part * width, width)
        for side, (source, target) in enumerate(((q_ref, q_out), (g_ref, g_out))):
            copies.append(pltpu.make_async_copy(source.at[:, cols], target.at[:, cols], sems.at[2 * part + side]))
    for copy in halves + copies:
        copy.start()
    for part in range(HK):
        for side, (source, target) in enumerate(((q_out, qt_ref), (g_out, gt_ref))):
            copies[2 * part + side].wait()
            for h in range(group):
                cols = slice(part * width + h * HD, part * width + (h + 1) * HD)
                target[:, cols] = jnp.transpose(source[:, cols])
    for copy in halves:
        copy.wait()


def score_kernel(group, tokens, scale, known, offset, q_ref, g_ref, qt_ref, gt_ref, own_ref, two_ref, one_ref, *refs):
    p_ref, ds_ref, far_ref, near_ref = refs[1:] if known else refs[:-1]
    bias_ref = refs[0] if known else refs[-1]
    tri = sees_own(tokens, 1)
    if not known:
        ids = own_ref.shape[0] - SEG_ROWS
        seg_query = segments(own_ref, ids, tokens)
        seg_own = jnp.transpose(seg_query)
        seg_one = jnp.transpose(segments(one_ref, ids, tokens))
        seg_two = jnp.transpose(segments(two_ref, ids, tokens))
        mixed = jnp.where(tri, seg_own, seg_two)
        bias_ref[0:tokens, :] = jnp.where(mixed == seg_query, 0.0, NEG)
        bias_ref[tokens : 2 * tokens, :] = jnp.where(seg_one == seg_query, 0.0, NEG)
    wide = UNIT * HD
    tri = sees_own(tokens, UNIT)
    far_mask = jnp.where(tri, 0.0, 1.0).astype(jnp.bfloat16)
    bias_mix = jnp.concatenate([bias_ref[0:tokens, :]] * UNIT, axis=1)
    bias_one = jnp.concatenate([bias_ref[tokens : 2 * tokens, :]] * UNIT, axis=1)
    factor = scale * LOG2E
    units = group // UNIT
    count = HK // CHUNKS

    def products(unit):
        part = unit // units
        keys, vals = [
            jnp.concatenate([ref[first : first + tokens, :] for ref in (own_ref, one_ref, two_ref)], axis=0)
            for first in (part * tokens, (count + part) * tokens)
        ]
        first = offset * group * HD + unit * wide
        return dot(keys, qt_ref[:, first : first + wide]), dot(vals, gt_ref[:, first : first + wide])

    ahead = products(0)
    for part in range(count):
        sum_k = jnp.zeros((2 * tokens, HD), jnp.float32)
        sum_v = jnp.zeros((2 * tokens, HD), jnp.float32)
        for step in range(units):
            unit = part * units + step
            raw, dp = ahead
            if unit + 1 < count * units:
                ahead = products(unit + 1)
            cols = slice(unit * wide, (unit + 1) * wide)
            s_mix = jnp.where(tri, raw[0:tokens], raw[2 * tokens :]) + bias_mix
            s_one = raw[tokens : 2 * tokens] + bias_one
            top = jnp.max(jnp.maximum(s_mix, s_one), axis=0, keepdims=True)
            e_mix = jnp.exp2((s_mix - top) * factor)
            e_one = jnp.exp2((s_one - top) * factor)
            d_mix = jnp.where(tri, dp[0:tokens], dp[2 * tokens :])
            d_one = dp[tokens : 2 * tokens]
            inverse = 1.0 / jnp.sum(e_mix + e_one, axis=0, keepdims=True)
            delta = jnp.sum(e_mix * d_mix + e_one * d_one, axis=0, keepdims=True) * inverse
            p_mix = e_mix * inverse
            p_one = e_one * inverse
            ds_mix = (p_mix * (d_mix - delta)).astype(jnp.bfloat16)
            ds_one = (p_one * (d_one - delta)).astype(jnp.bfloat16)
            p_mix = p_mix.astype(jnp.bfloat16)
            p_one = p_one.astype(jnp.bfloat16)
            p_ref[:, cols] = p_mix
            ds_ref[0:tokens, cols] = ds_mix
            ds_ref[tokens : 2 * tokens, cols] = ds_one
            first = offset * group + unit * UNIT
            sum_k = sum_k + dot(jnp.concatenate([ds_one, ds_mix * far_mask], axis=0), stacked(q_ref, first, UNIT))
            sum_v = sum_v + dot(jnp.concatenate([p_one, p_mix * far_mask], axis=0), stacked(g_ref, first, UNIT))
        sum_k = sum_k * scale
        cols = slice(part * HD, (part + 1) * HD)
        for ref, row in ((near_ref, 0), (far_ref, tokens)):
            ref[0:tokens, cols] = sum_k[row : row + tokens].astype(ref.dtype)
            ref[tokens : 2 * tokens, cols] = sum_v[row : row + tokens].astype(ref.dtype)


def leave(total, index, tokens, kv_ref, k_out, v_out, sems):
    width = total.shape[1]
    kv_ref[...] = total.astype(kv_ref.dtype)
    copies = [
        pltpu.make_async_copy(
            kv_ref.at[pl.ds(half * tokens, tokens), :], out.at[:, pl.ds(index * width, width)], sems.at[half]
        )
        for half, out in enumerate((k_out, v_out))
    ]
    for copy in copies:
        copy.start()
    return copies


def rest_kernel(group, tokens, scale, q_ref, g_ref, far_ref, near_ref, *refs):
    per = 5
    chunk_refs = [refs[per * c : per * (c + 1)] for c in range(CHUNKS)]
    dq_out, k_out, v_out, own_out, dq_ref, kv_ref, sems, kv_sems = refs[per * CHUNKS :]
    tri = sees_own(tokens, 2)
    own_mask = jnp.where(tri, 1.0, 0.0).astype(jnp.bfloat16)
    far_mask = jnp.where(tri, 0.0, 1.0).astype(jnp.bfloat16)
    wide = group * HD
    count = HK // CHUNKS
    copies = []
    for chunk, (p_ref, ds_ref, own_ref, two_ref, one_ref) in enumerate(chunk_refs):
        sums = []
        for part in range(count):
            block = slice(part * tokens, (part + 1) * tokens)
            keys_t = jnp.concatenate([jnp.transpose(ref[block, :]) for ref in (own_ref, one_ref, two_ref)], axis=1)
            sum_k = jnp.zeros((tokens, HD), jnp.float32)
            sum_v = jnp.zeros((tokens, HD), jnp.float32)
            for pair in range(group // 2):
                cols = slice(part * wide + pair * 2 * HD, part * wide + (pair + 1) * 2 * HD)
                first = (chunk * count + part) * group + 2 * pair
                ds_mix = ds_ref[0:tokens, cols]
                ds_own = ds_mix * own_mask
                sum_k = sum_k + dot(ds_own, stacked(q_ref, first, 2))
                sum_v = sum_v + dot(p_ref[:, cols] * own_mask, stacked(g_ref, first, 2))
                rows = jnp.concatenate([ds_own, ds_ref[tokens : 2 * tokens, cols], ds_mix * far_mask], axis=0)
                dq_t = (dot(keys_t, rows) * scale).astype(jnp.bfloat16)
                for h in range(2):
                    dq_ref[:, (first + h) * HD : (first + h + 1) * HD] = jnp.transpose(
                        dq_t[:, h * HD : (h + 1) * HD]
                    )
            sums.append(jnp.concatenate([sum_k * scale, sum_v], axis=0))
            index = chunk * count + part
            span = pl.ds(index * wide, wide)
            copies.append(pltpu.make_async_copy(dq_ref.at[:, span], dq_out.at[:, span], sems.at[index]))
            copies[-1].start()
        total = jnp.concatenate(sums, axis=1)
        if chunk == 0:
            total = total + near_ref[...].astype(jnp.float32) + far_ref[...].astype(jnp.float32)
            copies += leave(total, 0, tokens, kv_ref, k_out, v_out, kv_sems)
        else:
            own_out[...] = total
    for copy in copies:
        copy.wait()


def final_kernel(tokens, own_ref, far_ref, near_ref, k_before, v_before, k_out, v_out, kv_ref, sems):
    total = own_ref[...] + near_ref[...].astype(jnp.float32) + far_ref[...].astype(jnp.float32)
    for copy in leave(total, 1, tokens, kv_ref, k_out, v_out, sems):
        copy.wait()


def bf16(*shape):
    return jax.ShapeDtypeStruct(shape, jnp.bfloat16)


def f32(*shape):
    return jax.ShapeDtypeStruct(shape, jnp.float32)


def cost(flops, bytes_accessed, transcendentals=0):
    return pl.CostEstimate(flops=flops, bytes_accessed=bytes_accessed, transcendentals=transcendentals)


PARAMS = pltpu.CompilerParams(vmem_limit_bytes=VMEM_LIMIT)


def in_hbm(*arrays):
    return [pltpu.with_memory_space_constraint(x, pltpu.HBM) for x in arrays]


def pack_call(key_states, value_states, segment_ids):
    tokens, count = key_states.shape[0], HK // CHUNKS
    return pl.pallas_call(
        functools.partial(pack_kernel, tokens),
        in_specs=[pl.BlockSpec(memory_space=pltpu.HBM)] * 3,
        out_shape=bf16(2 * count * tokens + SEG_ROWS, HD),
        scratch_shapes=[
            pltpu.VMEM((tokens,), jnp.int32),
            pltpu.SemaphoreType.DMA((2 * count,)),
            pltpu.SemaphoreType.DMA((1,)),
        ],
        cost_estimate=cost(0, 8 * tokens * count * HD),
        compiler_params=PARAMS,
        name="pack",
    )(*in_hbm(key_states, value_states, segment_ids))


def turn_call(q, g, key_states, value_states, group):
    tokens, span = q.shape
    count = HK // CHUNKS
    return pl.pallas_call(
        functools.partial(turn_kernel, group),
        in_specs=[pl.BlockSpec(memory_space=pltpu.HBM)] * 4,
        out_shape=[bf16(tokens, span)] * 2 + [bf16(HD, span)] * 2 + [bf16(2 * count * tokens, HD)],
        scratch_shapes=[pltpu.SemaphoreType.DMA((2 * HK,)), pltpu.SemaphoreType.DMA((2 * count,))],
        cost_estimate=cost(0, 16 * tokens * span),
        compiler_params=PARAMS,
        name="turn",
    )(*in_hbm(q, g, key_states, value_states))


def score_call(q, g, qt, gt, own, two, one, bias, offset, group, tokens, scale):
    count = HK // CHUNKS
    span = count * group * HD
    known = bias is not None
    return pl.pallas_call(
        functools.partial(score_kernel, group, tokens, scale, known, offset),
        out_shape=[
            bf16(tokens, span),
            bf16(2 * tokens, span),
            bf16(2 * tokens, count * HD),
            bf16(2 * tokens, count * HD),
        ]
        + [f32(2 * tokens, tokens)] * (not known),
        cost_estimate=cost(2 * tokens * 3 * span * tokens * 4, 12 * tokens * span, 2 * tokens * span),
        compiler_params=PARAMS,
        name="scores",
    )(q, g, qt, gt, own, two, one, *([bias] if known else []))


ON_CHIP = pl.BlockSpec(memory_space=pltpu.VMEM)
IN_HBM = pl.BlockSpec(memory_space=pltpu.HBM)


def rest_call(q, g, far, near, parts, group, tokens, scale):
    grads = bf16(tokens, HK * HD)
    chunk = (2 * tokens, HK // CHUNKS * HD)
    return pl.pallas_call(
        functools.partial(rest_kernel, group, tokens, scale),
        out_specs=[IN_HBM] * 3 + [ON_CHIP],
        out_shape=[bf16(*q.shape), grads, grads, f32(*chunk)],
        scratch_shapes=[
            pltpu.VMEM(q.shape, jnp.bfloat16),
            pltpu.VMEM(chunk, jnp.bfloat16),
            pltpu.SemaphoreType.DMA((HK,)),
            pltpu.SemaphoreType.DMA((2,)),
        ],
        cost_estimate=cost(2 * tokens * 3 * q.shape[1] * tokens * 2, 12 * tokens * q.shape[1]),
        compiler_params=PARAMS,
        name="rest",
    )(q, g, far, near, *[x for part in parts for x in part])


def final_call(own, far, near, key_grad, value_grad):
    return pl.pallas_call(
        functools.partial(final_kernel, key_grad.shape[0]),
        in_specs=[ON_CHIP] * 3 + [IN_HBM] * 2,
        out_specs=[IN_HBM] * 2,
        out_shape=[bf16(*key_grad.shape)] * 2,
        scratch_shapes=[pltpu.VMEM(own.shape, jnp.bfloat16), pltpu.SemaphoreType.DMA((2,))],
        input_output_aliases={3: 0, 4: 1},
        cost_estimate=cost(0, 16 * own.shape[0] * own.shape[1]),
        compiler_params=PARAMS,
        name="final",
    )(own, far, near, key_grad, value_grad)


def shards(queries, key_states, value_states, out_grad, segment_ids):
    tokens = queries.shape[0]
    group = queries.shape[1] // (HK * HD)
    scale = HD ** (-0.5)
    chunks = range(CHUNKS)
    step = HK // CHUNKS
    own = [pack_call(key_states, value_states, segment_ids)]
    q, g, qt, gt, later = turn_call(queries, out_grad, key_states, value_states, group)
    own.append(later)
    two = [shift(x, 2) for x in own]
    one = [shift(x, 1) for x in own]
    first, near, far, bias = [], [], [], None
    for c in chunks:
        results = score_call(q, g, qt, gt, own[c], two[c], one[c], bias, c * step, group, tokens, scale)
        bias = results[4] if bias is None else bias
        first.append(results)
        far.append(shift(results[2], -2))
        near.append(shift(results[3], -1))
    query_grad, key_grad, value_grad, own_terms = rest_call(
        q, g, far[0], near[0], [(first[c][0], first[c][1], own[c], two[c], one[c]) for c in chunks],
        group, tokens, scale,
    )
    key_grad, value_grad = final_call(own_terms, far[1], near[1], key_grad, value_grad)
    return query_grad, key_grad, value_grad


def solution(mesh):
    rows = P(AXES, None)
    return jax.shard_map(
        shards,
        mesh=mesh,
        in_specs=(rows, rows, rows, rows, P(AXES)),
        out_specs=(rows, rows, rows),
        check_vma=False,
    )
```

```python
import functools

import jax
import jax.numpy as jnp
from jax import lax
from jax.experimental import pallas as pl
from jax.experimental.pallas import tpu as pltpu
from jax.sharding import PartitionSpec as P

HK = 4
HD = 128
SEG_ROWS = 16
NEG = -1e30
LOG2E = 1.4426950408889634
AXES = ("inner", "outer")
CHUNKS = 2
UNIT = 4
VMEM_LIMIT = 24 * 1024 * 1024


def shift(value, steps):
    count = lax.axis_size(AXES)
    first, last = max(0, -steps), min(count, count - steps)
    return lax.ppermute(value, AXES, [(i, i + steps) for i in range(first, last)])


def dot(a, b):
    return jnp.dot(a, b, preferred_element_type=jnp.float32)


def stacked(ref, first, count):
    return jnp.concatenate(
        [ref[:, (first + h) * HD : (first + h + 1) * HD] for h in range(count)], axis=0
    )


def sees_own(tokens, copies):
    key = lax.broadcasted_iota(jnp.int32, (tokens, tokens), 0)
    query = lax.broadcasted_iota(jnp.int32, (tokens, tokens), 1)
    return jnp.concatenate([key <= query] * copies, axis=1)


def segments(ref, first, tokens):
    coded = ref[first : first + SEG_ROWS, :].astype(jnp.float32)
    row = coded[0:1] * 2.0 + coded[1:2]
    return jnp.broadcast_to(row, (tokens, tokens))


def payload_copies(chunk, tokens, k_ref, v_ref, out_ref, sems):
    count = HK // CHUNKS
    return [
        pltpu.make_async_copy(
            source.at[:, pl.ds((chunk * count + part) * HD, HD)],
            out_ref.at[pl.ds((half * count + part) * tokens, tokens), :],
            sems.at[half * count + part],
        )
        for half, source in enumerate((k_ref, v_ref))
        for part in range(count)
    ]


def pack_kernel(tokens, k_ref, v_ref, seg_ref, out_ref, seg_own, sems, seg_sem):
    ids = pltpu.make_async_copy(seg_ref, seg_own, seg_sem.at[0])
    ids.start()
    copies = payload_copies(0, tokens, k_ref, v_ref, out_ref, sems)
    for copy in copies:
        copy.start()
    ids.wait()
    seg = jnp.broadcast_to((seg_own[...] + 1)[None, :], (SEG_ROWS, tokens))
    row = lax.broadcasted_iota(jnp.int32, (SEG_ROWS, tokens), 0)
    coded = jnp.where(row == 0, seg >> 1, jnp.where(row == 1, seg & 1, 0))
    first = out_ref.shape[0] - SEG_ROWS
    out_ref[first : first + SEG_ROWS, :] = coded.astype(jnp.float32).astype(jnp.bfloat16)
    for copy in copies:
        copy.wait()


def turn_kernel(group, chunk, q_ref, g_ref, *refs):
    halves = []
    if chunk == 0:
        k_ref, v_ref, q_out, g_out, qt_ref, gt_ref, kv_out, sems, kv_sems = refs
        halves = payload_copies(1, q_ref.shape[0], k_ref, v_ref, kv_out, kv_sems)
    else:
        q_out, g_out, qt_ref, gt_ref, sems = refs
    width = group * HD
    count = HK // CHUNKS
    copies = []
    for part in range(count):
        there = pl.ds((chunk * count + part) * width, width)
        here = pl.ds(part * width, width)
        for side, (source, target) in enumerate(((q_ref, q_out), (g_ref, g_out))):
            copies.append(pltpu.make_async_copy(source.at[:, there], target.at[:, here], sems.at[2 * part + side]))
    for copy in halves + copies:
        copy.start()
    for part in range(count):
        for side, (source, target) in enumerate(((q_out, qt_ref), (g_out, gt_ref))):
            copies[2 * part + side].wait()
            for h in range(group):
                cols = slice(part * width + h * HD, part * width + (h + 1) * HD)
                target[:, cols] = jnp.transpose(source[:, cols])
    for copy in halves:
        copy.wait()


def score_kernel(group, tokens, scale, known, q_ref, g_ref, qt_ref, gt_ref, own_ref, one_ref, two_ref, *refs):
    p_ref, ds_ref, far_ref, near_ref = refs[1:] if known else refs[:-1]
    bias_ref = refs[0] if known else refs[-1]
    tri = sees_own(tokens, 1)
    if not known:
        ids = own_ref.shape[0] - SEG_ROWS
        seg_query = segments(own_ref, ids, tokens)
        seg_own = jnp.transpose(seg_query)
        seg_one = jnp.transpose(segments(one_ref, ids, tokens))
        seg_two = jnp.transpose(segments(two_ref, ids, tokens))
        mixed = jnp.where(tri, seg_own, seg_two)
        bias_ref[0:tokens, :] = jnp.where(mixed == seg_query, 0.0, NEG)
        bias_ref[tokens : 2 * tokens, :] = jnp.where(seg_one == seg_query, 0.0, NEG)
    wide = UNIT * HD
    tri = sees_own(tokens, UNIT)
    far_mask = jnp.where(tri, 0.0, 1.0).astype(jnp.bfloat16)
    bias_mix = jnp.concatenate([bias_ref[0:tokens, :]] * UNIT, axis=1)
    bias_one = jnp.concatenate([bias_ref[tokens : 2 * tokens, :]] * UNIT, axis=1)
    factor = scale * LOG2E
    units = group // UNIT
    count = HK // CHUNKS

    def products(unit):
        part = unit // units
        keys, vals = [
            jnp.concatenate([ref[first : first + tokens, :] for ref in (own_ref, one_ref, two_ref)], axis=0)
            for first in (part * tokens, (count + part) * tokens)
        ]
        first = unit * wide
        return dot(keys, qt_ref[:, first : first + wide]), dot(vals, gt_ref[:, first : first + wide])

    ahead = products(0)
    for part in range(count):
        sum_k = jnp.zeros((2 * tokens, HD), jnp.float32)
        sum_v = jnp.zeros((2 * tokens, HD), jnp.float32)
        for step in range(units):
            unit = part * units + step
            raw, dp = ahead
            if unit + 1 < count * units:
                ahead = products(unit + 1)
            cols = slice(unit * wide, (unit + 1) * wide)
            s_mix = jnp.where(tri, raw[0:tokens], raw[2 * tokens :]) + bias_mix
            s_one = raw[tokens : 2 * tokens] + bias_one
            top = jnp.max(jnp.maximum(s_mix, s_one), axis=0, keepdims=True)
            e_mix = jnp.exp2((s_mix - top) * factor)
            e_one = jnp.exp2((s_one - top) * factor)
            d_mix = jnp.where(tri, dp[0:tokens], dp[2 * tokens :])
            d_one = dp[tokens : 2 * tokens]
            inverse = 1.0 / jnp.sum(e_mix + e_one, axis=0, keepdims=True)
            delta = jnp.sum(e_mix * d_mix + e_one * d_one, axis=0, keepdims=True) * inverse
            p_mix = e_mix * inverse
            p_one = e_one * inverse
            ds_mix = (p_mix * (d_mix - delta)).astype(jnp.bfloat16)
            ds_one = (p_one * (d_one - delta)).astype(jnp.bfloat16)
            p_mix = p_mix.astype(jnp.bfloat16)
            p_one = p_one.astype(jnp.bfloat16)
            p_ref[:, cols] = p_mix
            ds_ref[0:tokens, cols] = ds_mix
            ds_ref[tokens : 2 * tokens, cols] = ds_one
            first = unit * UNIT
            sum_k = sum_k + dot(jnp.concatenate([ds_one, ds_mix * far_mask], axis=0), stacked(q_ref, first, UNIT))
            sum_v = sum_v + dot(jnp.concatenate([p_one, p_mix * far_mask], axis=0), stacked(g_ref, first, UNIT))
        sum_k = sum_k * scale
        cols = slice(part * HD, (part + 1) * HD)
        for ref, row in ((near_ref, 0), (far_ref, tokens)):
            ref[0:tokens, cols] = sum_k[row : row + tokens].astype(ref.dtype)
            ref[tokens : 2 * tokens, cols] = sum_v[row : row + tokens].astype(ref.dtype)


def leave(total, index, tokens, kv_ref, k_out, v_out, sems):
    width = total.shape[1]
    kv_ref[...] = total.astype(kv_ref.dtype)
    copies = [
        pltpu.make_async_copy(
            kv_ref.at[pl.ds(half * tokens, tokens), :], out.at[:, pl.ds(index * width, width)], sems.at[half]
        )
        for half, out in enumerate((k_out, v_out))
    ]
    for copy in copies:
        copy.start()
    return copies


def rest_kernel(group, tokens, scale, far_ref, near_ref, *refs):
    per = 7
    chunk_refs = [refs[per * c : per * (c + 1)] for c in range(CHUNKS)]
    dq_out, k_out, v_out, own_out, dq_ref, kv_ref, sems, kv_sems = refs[per * CHUNKS :]
    tri = sees_own(tokens, 2)
    own_mask = jnp.where(tri, 1.0, 0.0).astype(jnp.bfloat16)
    far_mask = jnp.where(tri, 0.0, 1.0).astype(jnp.bfloat16)
    wide = group * HD
    count = HK // CHUNKS
    copies = []
    for chunk, (q_ref, g_ref, p_ref, ds_ref, own_ref, two_ref, one_ref) in enumerate(chunk_refs):
        sums = []
        for part in range(count):
            block = slice(part * tokens, (part + 1) * tokens)
            keys_t = jnp.concatenate([jnp.transpose(ref[block, :]) for ref in (own_ref, one_ref, two_ref)], axis=1)
            sum_k = jnp.zeros((tokens, HD), jnp.float32)
            sum_v = jnp.zeros((tokens, HD), jnp.float32)
            for pair in range(group // 2):
                cols = slice(part * wide + pair * 2 * HD, part * wide + (pair + 1) * 2 * HD)
                first = part * group + 2 * pair
                ds_mix = ds_ref[0:tokens, cols]
                ds_own = ds_mix * own_mask
                sum_k = sum_k + dot(ds_own, stacked(q_ref, first, 2))
                sum_v = sum_v + dot(p_ref[:, cols] * own_mask, stacked(g_ref, first, 2))
                rows = jnp.concatenate([ds_own, ds_ref[tokens : 2 * tokens, cols], ds_mix * far_mask], axis=0)
                dq_t = (dot(keys_t, rows) * scale).astype(jnp.bfloat16)
                for h in range(2):
                    at = (chunk * count * group + first + h) * HD
                    dq_ref[:, at : at + HD] = jnp.transpose(dq_t[:, h * HD : (h + 1) * HD])
            sums.append(jnp.concatenate([sum_k * scale, sum_v], axis=0))
            index = chunk * count + part
            span = pl.ds(index * wide, wide)
            copies.append(pltpu.make_async_copy(dq_ref.at[:, span], dq_out.at[:, span], sems.at[index]))
            copies[-1].start()
        total = jnp.concatenate(sums, axis=1)
        if chunk == 0:
            total = total + near_ref[...].astype(jnp.float32) + far_ref[...].astype(jnp.float32)
            copies += leave(total, 0, tokens, kv_ref, k_out, v_out, kv_sems)
        else:
            own_out[...] = total
    for copy in copies:
        copy.wait()


def final_kernel(tokens, own_ref, far_ref, near_ref, k_before, v_before, k_out, v_out, kv_ref, sems):
    total = own_ref[...] + near_ref[...].astype(jnp.float32) + far_ref[...].astype(jnp.float32)
    for copy in leave(total, 1, tokens, kv_ref, k_out, v_out, sems):
        copy.wait()


def bf16(*shape):
    return jax.ShapeDtypeStruct(shape, jnp.bfloat16)


def f32(*shape):
    return jax.ShapeDtypeStruct(shape, jnp.float32)


def cost(flops, bytes_accessed, transcendentals=0):
    return pl.CostEstimate(flops=flops, bytes_accessed=bytes_accessed, transcendentals=transcendentals)


PARAMS = pltpu.CompilerParams(vmem_limit_bytes=VMEM_LIMIT)


def in_hbm(*arrays):
    return [pltpu.with_memory_space_constraint(x, pltpu.HBM) for x in arrays]


def pack_call(key_states, value_states, segment_ids):
    tokens, count = key_states.shape[0], HK // CHUNKS
    return pl.pallas_call(
        functools.partial(pack_kernel, tokens),
        in_specs=[pl.BlockSpec(memory_space=pltpu.HBM)] * 3,
        out_shape=bf16(2 * count * tokens + SEG_ROWS, HD),
        scratch_shapes=[
            pltpu.VMEM((tokens,), jnp.int32),
            pltpu.SemaphoreType.DMA((2 * count,)),
            pltpu.SemaphoreType.DMA((1,)),
        ],
        cost_estimate=cost(0, 8 * tokens * count * HD),
        compiler_params=PARAMS,
        name="pack",
    )(*in_hbm(key_states, value_states, segment_ids))


def turn_call(chunk, group, q, g, *key_value):
    tokens, count = q.shape[0], HK // CHUNKS
    span = count * group * HD
    return pl.pallas_call(
        functools.partial(turn_kernel, group, chunk),
        in_specs=[pl.BlockSpec(memory_space=pltpu.HBM)] * (2 + len(key_value)),
        out_shape=[bf16(tokens, span)] * 2
        + [bf16(HD, span)] * 2
        + [bf16(2 * count * tokens, HD)] * (len(key_value) // 2),
        scratch_shapes=[pltpu.SemaphoreType.DMA((2 * count,))] * (1 + len(key_value) // 2),
        cost_estimate=cost(0, 16 * tokens * span),
        compiler_params=PARAMS,
        name="turn",
    )(*in_hbm(q, g, *key_value))


def score_call(q, g, qt, gt, own, one, two, bias, group, tokens, scale):
    count = HK // CHUNKS
    span = count * group * HD
    known = bias is not None
    return pl.pallas_call(
        functools.partial(score_kernel, group, tokens, scale, known),
        out_shape=[
            bf16(tokens, span),
            bf16(2 * tokens, span),
            bf16(2 * tokens, count * HD),
            bf16(2 * tokens, count * HD),
        ]
        + [f32(2 * tokens, tokens)] * (not known),
        cost_estimate=cost(2 * tokens * 3 * span * tokens * 4, 12 * tokens * span, 2 * tokens * span),
        compiler_params=PARAMS,
        name="scores",
    )(q, g, qt, gt, own, one, two, *([bias] if known else []))


ON_CHIP = pl.BlockSpec(memory_space=pltpu.VMEM)
IN_HBM = pl.BlockSpec(memory_space=pltpu.HBM)


def rest_call(far, near, parts, group, tokens, scale):
    grads = bf16(tokens, HK * HD)
    span = HK * group * HD
    chunk = (2 * tokens, HK // CHUNKS * HD)
    return pl.pallas_call(
        functools.partial(rest_kernel, group, tokens, scale),
        out_specs=[IN_HBM] * 3 + [ON_CHIP],
        out_shape=[bf16(tokens, span), grads, grads, f32(*chunk)],
        scratch_shapes=[
            pltpu.VMEM((tokens, span), jnp.bfloat16),
            pltpu.VMEM(chunk, jnp.bfloat16),
            pltpu.SemaphoreType.DMA((HK,)),
            pltpu.SemaphoreType.DMA((2,)),
        ],
        cost_estimate=cost(2 * tokens * 3 * span * tokens * 2, 12 * tokens * span),
        compiler_params=PARAMS,
        name="rest",
    )(far, near, *[x for part in parts for x in part])


def final_call(own, far, near, key_grad, value_grad):
    return pl.pallas_call(
        functools.partial(final_kernel, key_grad.shape[0]),
        in_specs=[ON_CHIP] * 3 + [IN_HBM] * 2,
        out_specs=[IN_HBM] * 2,
        out_shape=[bf16(*key_grad.shape)] * 2,
        scratch_shapes=[pltpu.VMEM(own.shape, jnp.bfloat16), pltpu.SemaphoreType.DMA((2,))],
        input_output_aliases={3: 0, 4: 1},
        cost_estimate=cost(0, 16 * own.shape[0] * own.shape[1]),
        compiler_params=PARAMS,
        name="final",
    )(own, far, near, key_grad, value_grad)


def shards(queries, key_states, value_states, out_grad, segment_ids):
    tokens = queries.shape[0]
    group = queries.shape[1] // (HK * HD)
    scale = HD ** (-0.5)
    chunks = range(CHUNKS)
    own = [pack_call(key_states, value_states, segment_ids)]
    *turned, later = turn_call(0, group, queries, out_grad, key_states, value_states)
    own.append(later)
    two = [shift(x, 2) for x in own]
    one = [shift(x, 1) for x in own]
    sides, first, near, far, bias = [], [], [], [], None
    for c in chunks:
        sides.append(turned)
        results = score_call(*turned, own[c], one[c], two[c], bias, group, tokens, scale)
        if c == 0:
            bias, queries, out_grad = lax.optimization_barrier((results[4], queries, out_grad))
            turned = turn_call(1, group, queries, out_grad)
        first.append(results)
        far.append(shift(results[2], -2))
        near.append(shift(results[3], -1))
    query_grad, key_grad, value_grad, own_terms = rest_call(
        far[0], near[0],
        [(sides[c][0], sides[c][1], first[c][0], first[c][1], own[c], two[c], one[c]) for c in chunks],
        group, tokens, scale,
    )
    key_grad, value_grad = final_call(own_terms, far[1], near[1], key_grad, value_grad)
    return query_grad, key_grad, value_grad


def solution(mesh):
    rows = P(AXES, None)
    return jax.shard_map(
        shards,
        mesh=mesh,
        in_specs=(rows, rows, rows, rows, P(AXES)),
        out_specs=(rows, rows, rows),
        check_vma=False,
    )
```

```python
import functools

import jax
import jax.numpy as jnp
from jax import lax
from jax.experimental import pallas as pl
from jax.experimental.pallas import tpu as pltpu
from jax.sharding import PartitionSpec as P

HK = 4
HD = 128
SEG_ROWS = 16
NEG = -1e30
LOG2E = 1.4426950408889634
AXES = ("inner", "outer")
CHUNKS = 2
UNIT = 4
VMEM_LIMIT = 24 * 1024 * 1024


def shift(value, steps):
    count = lax.axis_size(AXES)
    first, last = max(0, -steps), min(count, count - steps)
    return lax.ppermute(value, AXES, [(i, i + steps) for i in range(first, last)])


def dot(a, b):
    return jnp.dot(a, b, preferred_element_type=jnp.float32)


def stacked(ref, first, count):
    return jnp.concatenate(
        [ref[:, (first + h) * HD : (first + h + 1) * HD] for h in range(count)], axis=0
    )


def sees_own(tokens, copies):
    key = lax.broadcasted_iota(jnp.int32, (tokens, tokens), 0)
    query = lax.broadcasted_iota(jnp.int32, (tokens, tokens), 1)
    return jnp.concatenate([key <= query] * copies, axis=1)


def segments(ref, first, tokens):
    coded = ref[first : first + SEG_ROWS, :].astype(jnp.float32)
    row = coded[0:1] * 2.0 + coded[1:2]
    return jnp.broadcast_to(row, (tokens, tokens))


def payload_copies(chunk, tokens, k_ref, v_ref, out_ref, sems):
    count = HK // CHUNKS
    return [
        pltpu.make_async_copy(
            source.at[:, pl.ds((chunk * count + part) * HD, HD)],
            out_ref.at[pl.ds((half * count + part) * tokens, tokens), :],
            sems.at[half * count + part],
        )
        for half, source in enumerate((k_ref, v_ref))
        for part in range(count)
    ]


def pack_kernel(tokens, k_ref, v_ref, seg_ref, out_ref, seg_own, sems, seg_sem):
    ids = pltpu.make_async_copy(seg_ref, seg_own, seg_sem.at[0])
    ids.start()
    copies = payload_copies(0, tokens, k_ref, v_ref, out_ref, sems)
    for copy in copies:
        copy.start()
    ids.wait()
    seg = jnp.broadcast_to((seg_own[...] + 1)[None, :], (SEG_ROWS, tokens))
    row = lax.broadcasted_iota(jnp.int32, (SEG_ROWS, tokens), 0)
    coded = jnp.where(row == 0, seg >> 1, jnp.where(row == 1, seg & 1, 0))
    first = out_ref.shape[0] - SEG_ROWS
    out_ref[first : first + SEG_ROWS, :] = coded.astype(jnp.float32).astype(jnp.bfloat16)
    for copy in copies:
        copy.wait()


def turn_kernel(group, q_ref, g_ref, k_ref, v_ref, q_out, g_out, qt_ref, gt_ref, kv_out, sems, kv_sems):
    width = group * HD
    halves = payload_copies(1, q_ref.shape[0], k_ref, v_ref, kv_out, kv_sems)
    copies = []
    for part in range(HK):
        cols = pl.ds(part * width, width)
        for side, (source, target) in enumerate(((q_ref, q_out), (g_ref, g_out))):
            copies.append(pltpu.make_async_copy(source.at[:, cols], target.at[:, cols], sems.at[2 * part + side]))
    for copy in halves + copies:
        copy.start()
    for part in range(HK):
        for side, (source, target) in enumerate(((q_out, qt_ref), (g_out, gt_ref))):
            copies[2 * part + side].wait()
            for h in range(group):
                cols = slice(part * width + h * HD, part * width + (h + 1) * HD)
                target[:, cols] = jnp.transpose(source[:, cols])
    for copy in halves:
        copy.wait()


def score_kernel(group, tokens, scale, known, offset, q_ref, g_ref, qt_ref, gt_ref, own_ref, one_ref, two_ref, *refs):
    p_ref, ds_ref, far_ref, near_ref = refs[1:] if known else refs[:-1]
    bias_ref = refs[0] if known else refs[-1]
    tri = sees_own(tokens, 1)
    if not known:
        ids = own_ref.shape[0] - SEG_ROWS
        seg_query = segments(own_ref, ids, tokens)
        seg_own = jnp.transpose(seg_query)
        seg_one = jnp.transpose(segments(one_ref, ids, tokens))
        seg_two = jnp.transpose(segments(two_ref, ids, tokens))
        mixed = jnp.where(tri, seg_own, seg_two)
        bias_ref[0:tokens, :] = jnp.where(mixed == seg_query, 0.0, NEG)
        bias_ref[tokens : 2 * tokens, :] = jnp.where(seg_one == seg_query, 0.0, NEG)
    wide = UNIT * HD
    tri = sees_own(tokens, UNIT)
    far_mask = jnp.where(tri, 0.0, 1.0).astype(jnp.bfloat16)
    bias_mix = jnp.concatenate([bias_ref[0:tokens, :]] * UNIT, axis=1)
    bias_one = jnp.concatenate([bias_ref[tokens : 2 * tokens, :]] * UNIT, axis=1)
    factor = scale * LOG2E
    units = group // UNIT
    count = HK // CHUNKS

    def products(unit):
        part = unit // units
        keys, vals = [
            jnp.concatenate([ref[first : first + tokens, :] for ref in (own_ref, one_ref, two_ref)], axis=0)
            for first in (part * tokens, (count + part) * tokens)
        ]
        first = offset * group * HD + unit * wide
        return dot(keys, qt_ref[:, first : first + wide]), dot(vals, gt_ref[:, first : first + wide])

    ahead = products(0)
    for part in range(count):
        sum_k = jnp.zeros((2 * tokens, HD), jnp.float32)
        sum_v = jnp.zeros((2 * tokens, HD), jnp.float32)
        for step in range(units):
            unit = part * units + step
            raw, dp = ahead
            if unit + 1 < count * units:
                ahead = products(unit + 1)
            cols = slice(unit * wide, (unit + 1) * wide)
            s_mix = jnp.where(tri, raw[0:tokens], raw[2 * tokens :]) + bias_mix
            s_one = raw[tokens : 2 * tokens] + bias_one
            top = jnp.max(jnp.maximum(s_mix, s_one), axis=0, keepdims=True)
            e_mix = jnp.exp2((s_mix - top) * factor)
            e_one = jnp.exp2((s_one - top) * factor)
            d_mix = jnp.where(tri, dp[0:tokens], dp[2 * tokens :])
            d_one = dp[tokens : 2 * tokens]
            inverse = 1.0 / jnp.sum(e_mix + e_one, axis=0, keepdims=True)
            delta = jnp.sum(e_mix * d_mix + e_one * d_one, axis=0, keepdims=True) * inverse
            p_mix = e_mix * inverse
            p_one = e_one * inverse
            ds_mix = (p_mix * (d_mix - delta)).astype(jnp.bfloat16)
            ds_one = (p_one * (d_one - delta)).astype(jnp.bfloat16)
            p_mix = p_mix.astype(jnp.bfloat16)
            p_one = p_one.astype(jnp.bfloat16)
            p_ref[:, cols] = p_mix
            ds_ref[0:tokens, cols] = ds_mix
            ds_ref[tokens : 2 * tokens, cols] = ds_one
            first = offset * group + unit * UNIT
            sum_k = sum_k + dot(jnp.concatenate([ds_one, ds_mix * far_mask], axis=0), stacked(q_ref, first, UNIT))
            sum_v = sum_v + dot(jnp.concatenate([p_one, p_mix * far_mask], axis=0), stacked(g_ref, first, UNIT))
        sum_k = sum_k * scale
        cols = slice(part * HD, (part + 1) * HD)
        for ref, row in ((near_ref, 0), (far_ref, tokens)):
            ref[0:tokens, cols] = sum_k[row : row + tokens].astype(ref.dtype)
            ref[tokens : 2 * tokens, cols] = sum_v[row : row + tokens].astype(ref.dtype)


def rest_kernel(group, tokens, scale, q_ref, g_ref, *refs):
    per = 5
    chunk_refs = [refs[per * c : per * (c + 1)] for c in range(CHUNKS)]
    dq_out, own_out, dq_ref, sems = refs[per * CHUNKS :]
    tri = sees_own(tokens, 2)
    own_mask = jnp.where(tri, 1.0, 0.0).astype(jnp.bfloat16)
    far_mask = jnp.where(tri, 0.0, 1.0).astype(jnp.bfloat16)
    wide = group * HD
    count = HK // CHUNKS
    copies = []
    for chunk, (p_ref, ds_ref, own_ref, two_ref, one_ref) in enumerate(chunk_refs):
        for part in range(count):
            block = slice(part * tokens, (part + 1) * tokens)
            keys_t = jnp.concatenate([jnp.transpose(ref[block, :]) for ref in (own_ref, one_ref, two_ref)], axis=1)
            sum_k = jnp.zeros((tokens, HD), jnp.float32)
            sum_v = jnp.zeros((tokens, HD), jnp.float32)
            for pair in range(group // 2):
                cols = slice(part * wide + pair * 2 * HD, part * wide + (pair + 1) * 2 * HD)
                first = (chunk * count + part) * group + 2 * pair
                ds_mix = ds_ref[0:tokens, cols]
                ds_own = ds_mix * own_mask
                sum_k = sum_k + dot(ds_own, stacked(q_ref, first, 2))
                sum_v = sum_v + dot(p_ref[:, cols] * own_mask, stacked(g_ref, first, 2))
                rows = jnp.concatenate([ds_own, ds_ref[tokens : 2 * tokens, cols], ds_mix * far_mask], axis=0)
                dq_t = (dot(keys_t, rows) * scale).astype(jnp.bfloat16)
                for h in range(2):
                    dq_ref[:, (first + h) * HD : (first + h + 1) * HD] = jnp.transpose(
                        dq_t[:, h * HD : (h + 1) * HD]
                    )
            total = jnp.concatenate([sum_k * scale, sum_v], axis=0)
            index = chunk * count + part
            own_out[:, index * HD : (index + 1) * HD] = total
            span = pl.ds(index * wide, wide)
            copies.append(pltpu.make_async_copy(dq_ref.at[:, span], dq_out.at[:, span], sems.at[index]))
            copies[-1].start()
    for copy in copies:
        copy.wait()


def join_kernel(first_ref, handed_ref, second_ref, out_ref):
    width = first_ref.shape[1]
    out_ref[:, 0:width] = (first_ref[...] + handed_ref[...].astype(jnp.float32)).astype(out_ref.dtype)
    out_ref[:, width:] = second_ref[...].astype(out_ref.dtype)


def final_kernel(tokens, own_ref, far_ref, near_ref, k_out, v_out):
    total = own_ref[...] + near_ref[...].astype(jnp.float32)
    width = far_ref.shape[1]
    total = jnp.concatenate([total[:, 0:width], total[:, width:] + far_ref[...].astype(jnp.float32)], axis=1)
    k_out[...] = total[0:tokens].astype(k_out.dtype)
    v_out[...] = total[tokens:].astype(v_out.dtype)


def bf16(*shape):
    return jax.ShapeDtypeStruct(shape, jnp.bfloat16)


def f32(*shape):
    return jax.ShapeDtypeStruct(shape, jnp.float32)


def cost(flops, bytes_accessed, transcendentals=0):
    return pl.CostEstimate(flops=flops, bytes_accessed=bytes_accessed, transcendentals=transcendentals)


PARAMS = pltpu.CompilerParams(vmem_limit_bytes=VMEM_LIMIT)


def in_hbm(*arrays):
    return [pltpu.with_memory_space_constraint(x, pltpu.HBM) for x in arrays]


def pack_call(key_states, value_states, segment_ids):
    tokens, count = key_states.shape[0], HK // CHUNKS
    return pl.pallas_call(
        functools.partial(pack_kernel, tokens),
        in_specs=[pl.BlockSpec(memory_space=pltpu.HBM)] * 3,
        out_shape=bf16(2 * count * tokens + SEG_ROWS, HD),
        scratch_shapes=[
            pltpu.VMEM((tokens,), jnp.int32),
            pltpu.SemaphoreType.DMA((2 * count,)),
            pltpu.SemaphoreType.DMA((1,)),
        ],
        cost_estimate=cost(0, 8 * tokens * count * HD),
        compiler_params=PARAMS,
        name="pack",
    )(*in_hbm(key_states, value_states, segment_ids))


def turn_call(q, g, key_states, value_states, group):
    tokens, span = q.shape
    count = HK // CHUNKS
    return pl.pallas_call(
        functools.partial(turn_kernel, group),
        in_specs=[pl.BlockSpec(memory_space=pltpu.HBM)] * 4,
        out_shape=[bf16(tokens, span)] * 2 + [bf16(HD, span)] * 2 + [bf16(2 * count * tokens, HD)],
        scratch_shapes=[pltpu.SemaphoreType.DMA((2 * HK,)), pltpu.SemaphoreType.DMA((2 * count,))],
        cost_estimate=cost(0, 16 * tokens * span),
        compiler_params=PARAMS,
        name="turn",
    )(*in_hbm(q, g, key_states, value_states))


def score_call(q, g, qt, gt, own, one, two, bias, offset, group, tokens, scale):
    count = HK // CHUNKS
    span = count * group * HD
    known = bias is not None
    return pl.pallas_call(
        functools.partial(score_kernel, group, tokens, scale, known, offset),
        out_shape=[
            bf16(tokens, span),
            bf16(2 * tokens, span),
            bf16(2 * tokens, count * HD),
            f32(2 * tokens, count * HD),
        ]
        + [f32(2 * tokens, tokens)] * (not known),
        cost_estimate=cost(2 * tokens * 3 * span * tokens * 4, 12 * tokens * span, 2 * tokens * span),
        compiler_params=PARAMS,
        name="scores",
    )(q, g, qt, gt, own, one, two, *([bias] if known else []))


def rest_call(q, g, parts, group, tokens, scale):
    return pl.pallas_call(
        functools.partial(rest_kernel, group, tokens, scale),
        out_specs=[pl.BlockSpec(memory_space=pltpu.HBM), pl.BlockSpec(memory_space=pltpu.VMEM)],
        out_shape=[bf16(*q.shape), f32(2 * tokens, HK * HD)],
        scratch_shapes=[pltpu.VMEM(q.shape, jnp.bfloat16), pltpu.SemaphoreType.DMA((HK,))],
        cost_estimate=cost(2 * tokens * 3 * q.shape[1] * tokens * 2, 12 * tokens * q.shape[1]),
        compiler_params=PARAMS,
        name="rest",
    )(q, g, *[x for part in parts for x in part])


def join_call(first, handed, second):
    rows, width = first.shape
    return pl.pallas_call(
        join_kernel,
        out_shape=bf16(rows, 2 * width),
        cost_estimate=cost(0, 12 * rows * width),
        compiler_params=PARAMS,
        name="join",
    )(first, handed, second)


def final_call(own, far, near):
    tokens, width = own.shape[0] // 2, own.shape[1]
    return pl.pallas_call(
        functools.partial(final_kernel, tokens),
        out_shape=[bf16(tokens, width)] * 2,
        cost_estimate=cost(0, 16 * tokens * width),
        compiler_params=PARAMS,
        name="final",
    )(own, far, near)


def shards(queries, key_states, value_states, out_grad, segment_ids):
    tokens = queries.shape[0]
    group = queries.shape[1] // (HK * HD)
    scale = HD ** (-0.5)
    chunks = range(CHUNKS)
    step = HK // CHUNKS
    own = [pack_call(key_states, value_states, segment_ids)]
    q, g, qt, gt, later = turn_call(queries, out_grad, key_states, value_states, group)
    own.append(later)
    two = [shift(x, 2) for x in own]
    one = [shift(x, 1) for x in own]
    first, bias = [], None
    for c in chunks:
        first.append(score_call(q, g, qt, gt, own[c], one[c], two[c], bias, c * step, group, tokens, scale))
        bias = first[0][4]
    handed = shift(first[0][2], -1)
    far = shift(first[1][2], -2)
    near = shift(join_call(first[0][3], handed, first[1][3]), -1)
    query_grad, own_terms = rest_call(
        q, g, [(first[c][0], first[c][1], own[c], two[c], one[c]) for c in chunks], group, tokens, scale
    )
    key_grad, value_grad = final_call(own_terms, far, near)
    return query_grad, key_grad, value_grad


def solution(mesh):
    rows = P(AXES, None)
    return jax.shard_map(
        shards,
        mesh=mesh,
        in_specs=(rows, rows, rows, rows, P(AXES)),
        out_specs=(rows, rows, rows),
        check_vma=False,
    )
```

```python
import functools

import jax
import jax.numpy as jnp
from jax import lax
from jax.experimental import pallas as pl
from jax.experimental.pallas import tpu as pltpu
from jax.sharding import PartitionSpec as P

HK = 4
HD = 128
SEG_ROWS = 16
NEG = -1e30
LOG2E = 1.4426950408889634
AXES = ("inner", "outer")
CHUNKS = 2
UNIT = 8
VMEM_LIMIT = 24 * 1024 * 1024


def shift(value, steps):
    count = lax.axis_size(AXES)
    first, last = max(0, -steps), min(count, count - steps)
    return lax.ppermute(value, AXES, [(i, i + steps) for i in range(first, last)])


def dot(a, b):
    return jnp.dot(a, b, preferred_element_type=jnp.float32)


def stacked(ref, first, count):
    return jnp.concatenate(
        [ref[:, (first + h) * HD : (first + h + 1) * HD] for h in range(count)], axis=0
    )


def sees_own(tokens, copies):
    key = lax.broadcasted_iota(jnp.int32, (tokens, tokens), 0)
    query = lax.broadcasted_iota(jnp.int32, (tokens, tokens), 1)
    return jnp.concatenate([key <= query] * copies, axis=1)


def segments(ref, first, tokens):
    coded = ref[first : first + SEG_ROWS, :].astype(jnp.float32)
    row = coded[0:1] * 2.0 + coded[1:2]
    return jnp.broadcast_to(row, (tokens, tokens))


def payload_copies(chunk, tokens, k_ref, v_ref, out_ref, sems):
    count = HK // CHUNKS
    return [
        pltpu.make_async_copy(
            source.at[:, pl.ds((chunk * count + part) * HD, HD)],
            out_ref.at[pl.ds((half * count + part) * tokens, tokens), :],
            sems.at[half * count + part],
        )
        for half, source in enumerate((k_ref, v_ref))
        for part in range(count)
    ]


def pack_kernel(tokens, k_ref, v_ref, seg_ref, out_ref, seg_own, sems, seg_sem):
    ids = pltpu.make_async_copy(seg_ref, seg_own, seg_sem.at[0])
    ids.start()
    copies = payload_copies(0, tokens, k_ref, v_ref, out_ref, sems)
    for copy in copies:
        copy.start()
    ids.wait()
    seg = jnp.broadcast_to((seg_own[...] + 1)[None, :], (SEG_ROWS, tokens))
    row = lax.broadcasted_iota(jnp.int32, (SEG_ROWS, tokens), 0)
    coded = jnp.where(row == 0, seg >> 1, jnp.where(row == 1, seg & 1, 0))
    first = out_ref.shape[0] - SEG_ROWS
    out_ref[first : first + SEG_ROWS, :] = coded.astype(jnp.float32).astype(jnp.bfloat16)
    for copy in copies:
        copy.wait()


def turn_kernel(group, q_ref, g_ref, k_ref, v_ref, q_out, g_out, qt_ref, gt_ref, kv_out, sems, kv_sems):
    width = group * HD
    halves = payload_copies(1, q_ref.shape[0], k_ref, v_ref, kv_out, kv_sems)
    copies = []
    for part in range(HK):
        cols = pl.ds(part * width, width)
        for side, (source, target) in enumerate(((q_ref, q_out), (g_ref, g_out))):
            copies.append(pltpu.make_async_copy(source.at[:, cols], target.at[:, cols], sems.at[2 * part + side]))
    for copy in halves + copies:
        copy.start()
    for part in range(HK):
        for side, (source, target) in enumerate(((q_out, qt_ref), (g_out, gt_ref))):
            copies[2 * part + side].wait()
            for h in range(group):
                cols = slice(part * width + h * HD, part * width + (h + 1) * HD)
                target[:, cols] = jnp.transpose(source[:, cols])
    for copy in halves:
        copy.wait()


def score_kernel(group, tokens, scale, known, offset, q_ref, g_ref, qt_ref, gt_ref, own_ref, two_ref, one_ref, *refs):
    p_ref, ds_ref, far_ref, near_ref = refs[1:] if known else refs[:-1]
    bias_ref = refs[0] if known else refs[-1]
    tri = sees_own(tokens, 1)
    if not known:
        ids = own_ref.shape[0] - SEG_ROWS
        seg_query = segments(own_ref, ids, tokens)
        seg_own = jnp.transpose(seg_query)
        seg_one = jnp.transpose(segments(one_ref, ids, tokens))
        seg_two = jnp.transpose(segments(two_ref, ids, tokens))
        mixed = jnp.where(tri, seg_own, seg_two)
        bias_ref[0:tokens, :] = jnp.where(mixed == seg_query, 0.0, NEG)
        bias_ref[tokens : 2 * tokens, :] = jnp.where(seg_one == seg_query, 0.0, NEG)
    wide = UNIT * HD
    tri = sees_own(tokens, UNIT)
    far_mask = jnp.where(tri, 0.0, 1.0).astype(jnp.bfloat16)
    bias_mix = jnp.concatenate([bias_ref[0:tokens, :]] * UNIT, axis=1)
    bias_one = jnp.concatenate([bias_ref[tokens : 2 * tokens, :]] * UNIT, axis=1)
    factor = scale * LOG2E
    units = group // UNIT
    count = HK // CHUNKS

    def products(unit):
        part = unit // units
        keys, vals = [
            jnp.concatenate([ref[first : first + tokens, :] for ref in (own_ref, one_ref, two_ref)], axis=0)
            for first in (part * tokens, (count + part) * tokens)
        ]
        first = offset * group * HD + unit * wide
        return dot(keys, qt_ref[:, first : first + wide]), dot(vals, gt_ref[:, first : first + wide])

    ahead = products(0)
    for part in range(count):
        sum_k = jnp.zeros((2 * tokens, HD), jnp.float32)
        sum_v = jnp.zeros((2 * tokens, HD), jnp.float32)
        for step in range(units):
            unit = part * units + step
            raw, dp = ahead
            if unit + 1 < count * units:
                ahead = products(unit + 1)
            cols = slice(unit * wide, (unit + 1) * wide)
            s_mix = jnp.where(tri, raw[0:tokens], raw[2 * tokens :]) + bias_mix
            s_one = raw[tokens : 2 * tokens] + bias_one
            top = jnp.max(jnp.maximum(s_mix, s_one), axis=0, keepdims=True)
            e_mix = jnp.exp2((s_mix - top) * factor)
            e_one = jnp.exp2((s_one - top) * factor)
            inverse = 1.0 / jnp.sum(e_mix + e_one, axis=0, keepdims=True)
            p_mix = e_mix * inverse
            p_one = e_one * inverse
            d_mix = jnp.where(tri, dp[0:tokens], dp[2 * tokens :])
            d_one = dp[tokens : 2 * tokens]
            delta = jnp.sum(p_mix * d_mix + p_one * d_one, axis=0, keepdims=True)
            ds_mix = (p_mix * (d_mix - delta)).astype(jnp.bfloat16)
            ds_one = (p_one * (d_one - delta)).astype(jnp.bfloat16)
            p_mix = p_mix.astype(jnp.bfloat16)
            p_one = p_one.astype(jnp.bfloat16)
            p_ref[:, cols] = p_mix
            ds_ref[0:tokens, cols] = ds_mix
            ds_ref[tokens : 2 * tokens, cols] = ds_one
            first = offset * group + unit * UNIT
            sum_k = sum_k + dot(jnp.concatenate([ds_one, ds_mix * far_mask], axis=0), stacked(q_ref, first, UNIT))
            sum_v = sum_v + dot(jnp.concatenate([p_one, p_mix * far_mask], axis=0), stacked(g_ref, first, UNIT))
        sum_k = sum_k * scale
        cols = slice(part * HD, (part + 1) * HD)
        for ref, row in ((near_ref, 0), (far_ref, tokens)):
            ref[0:tokens, cols] = sum_k[row : row + tokens].astype(ref.dtype)
            ref[tokens : 2 * tokens, cols] = sum_v[row : row + tokens].astype(ref.dtype)


def leave(total, index, tokens, kv_ref, k_out, v_out, sems):
    width = total.shape[1]
    kv_ref[...] = total.astype(kv_ref.dtype)
    copies = [
        pltpu.make_async_copy(
            kv_ref.at[pl.ds(half * tokens, tokens), :], out.at[:, pl.ds(index * width, width)], sems.at[half]
        )
        for half, out in enumerate((k_out, v_out))
    ]
    for copy in copies:
        copy.start()
    return copies


def rest_kernel(group, tokens, scale, q_ref, g_ref, far_ref, near_ref, *refs):
    per = 5
    chunk_refs = [refs[per * c : per * (c + 1)] for c in range(CHUNKS)]
    dq_out, k_out, v_out, own_out, dq_ref, kv_ref, sems, kv_sems = refs[per * CHUNKS :]
    tri = sees_own(tokens, 2)
    own_mask = jnp.where(tri, 1.0, 0.0).astype(jnp.bfloat16)
    far_mask = jnp.where(tri, 0.0, 1.0).astype(jnp.bfloat16)
    wide = group * HD
    count = HK // CHUNKS
    copies = []
    for chunk, (p_ref, ds_ref, own_ref, two_ref, one_ref) in enumerate(chunk_refs):
        sums = []
        for part in range(count):
            block = slice(part * tokens, (part + 1) * tokens)
            keys_t = jnp.concatenate([jnp.transpose(ref[block, :]) for ref in (own_ref, one_ref, two_ref)], axis=1)
            sum_k = jnp.zeros((tokens, HD), jnp.float32)
            sum_v = jnp.zeros((tokens, HD), jnp.float32)
            for pair in range(group // 2):
                cols = slice(part * wide + pair * 2 * HD, part * wide + (pair + 1) * 2 * HD)
                first = (chunk * count + part) * group + 2 * pair
                ds_mix = ds_ref[0:tokens, cols]
                ds_own = ds_mix * own_mask
                sum_k = sum_k + dot(ds_own, stacked(q_ref, first, 2))
                sum_v = sum_v + dot(p_ref[:, cols] * own_mask, stacked(g_ref, first, 2))
                rows = jnp.concatenate([ds_own, ds_ref[tokens : 2 * tokens, cols], ds_mix * far_mask], axis=0)
                dq_t = (dot(keys_t, rows) * scale).astype(jnp.bfloat16)
                for h in range(2):
                    dq_ref[:, (first + h) * HD : (first + h + 1) * HD] = jnp.transpose(
                        dq_t[:, h * HD : (h + 1) * HD]
                    )
            sums.append(jnp.concatenate([sum_k * scale, sum_v], axis=0))
            index = chunk * count + part
            span = pl.ds(index * wide, wide)
            copies.append(pltpu.make_async_copy(dq_ref.at[:, span], dq_out.at[:, span], sems.at[index]))
            copies[-1].start()
        total = jnp.concatenate(sums, axis=1)
        if chunk == 0:
            total = total + near_ref[...].astype(jnp.float32) + far_ref[...].astype(jnp.float32)
            copies += leave(total, 0, tokens, kv_ref, k_out, v_out, kv_sems)
        else:
            own_out[...] = total
    for copy in copies:
        copy.wait()


def final_kernel(tokens, own_ref, far_ref, near_ref, k_before, v_before, k_out, v_out, kv_ref, sems):
    total = own_ref[...] + near_ref[...].astype(jnp.float32) + far_ref[...].astype(jnp.float32)
    for copy in leave(total, 1, tokens, kv_ref, k_out, v_out, sems):
        copy.wait()


def bf16(*shape):
    return jax.ShapeDtypeStruct(shape, jnp.bfloat16)


def f32(*shape):
    return jax.ShapeDtypeStruct(shape, jnp.float32)


def cost(flops, bytes_accessed, transcendentals=0):
    return pl.CostEstimate(flops=flops, bytes_accessed=bytes_accessed, transcendentals=transcendentals)


PARAMS = pltpu.CompilerParams(vmem_limit_bytes=VMEM_LIMIT)


def in_hbm(*arrays):
    return [pltpu.with_memory_space_constraint(x, pltpu.HBM) for x in arrays]


def pack_call(key_states, value_states, segment_ids):
    tokens, count = key_states.shape[0], HK // CHUNKS
    return pl.pallas_call(
        functools.partial(pack_kernel, tokens),
        in_specs=[pl.BlockSpec(memory_space=pltpu.HBM)] * 3,
        out_shape=bf16(2 * count * tokens + SEG_ROWS, HD),
        scratch_shapes=[
            pltpu.VMEM((tokens,), jnp.int32),
            pltpu.SemaphoreType.DMA((2 * count,)),
            pltpu.SemaphoreType.DMA((1,)),
        ],
        cost_estimate=cost(0, 8 * tokens * count * HD),
        compiler_params=PARAMS,
        name="pack",
    )(*in_hbm(key_states, value_states, segment_ids))


def turn_call(q, g, key_states, value_states, group):
    tokens, span = q.shape
    count = HK // CHUNKS
    return pl.pallas_call(
        functools.partial(turn_kernel, group),
        in_specs=[pl.BlockSpec(memory_space=pltpu.HBM)] * 4,
        out_shape=[bf16(tokens, span)] * 2 + [bf16(HD, span)] * 2 + [bf16(2 * count * tokens, HD)],
        scratch_shapes=[pltpu.SemaphoreType.DMA((2 * HK,)), pltpu.SemaphoreType.DMA((2 * count,))],
        cost_estimate=cost(0, 16 * tokens * span),
        compiler_params=PARAMS,
        name="turn",
    )(*in_hbm(q, g, key_states, value_states))


def score_call(q, g, qt, gt, own, two, one, bias, offset, group, tokens, scale):
    count = HK // CHUNKS
    span = count * group * HD
    known = bias is not None
    return pl.pallas_call(
        functools.partial(score_kernel, group, tokens, scale, known, offset),
        out_shape=[
            bf16(tokens, span),
            bf16(2 * tokens, span),
            bf16(2 * tokens, count * HD),
            bf16(2 * tokens, count * HD),
        ]
        + [f32(2 * tokens, tokens)] * (not known),
        cost_estimate=cost(2 * tokens * 3 * span * tokens * 4, 12 * tokens * span, 2 * tokens * span),
        compiler_params=PARAMS,
        name="scores",
    )(q, g, qt, gt, own, two, one, *([bias] if known else []))


ON_CHIP = pl.BlockSpec(memory_space=pltpu.VMEM)
IN_HBM = pl.BlockSpec(memory_space=pltpu.HBM)


def rest_call(q, g, far, near, parts, group, tokens, scale):
    grads = bf16(tokens, HK * HD)
    chunk = (2 * tokens, HK // CHUNKS * HD)
    return pl.pallas_call(
        functools.partial(rest_kernel, group, tokens, scale),
        out_specs=[IN_HBM] * 3 + [ON_CHIP],
        out_shape=[bf16(*q.shape), grads, grads, f32(*chunk)],
        scratch_shapes=[
            pltpu.VMEM(q.shape, jnp.bfloat16),
            pltpu.VMEM(chunk, jnp.bfloat16),
            pltpu.SemaphoreType.DMA((HK,)),
            pltpu.SemaphoreType.DMA((2,)),
        ],
        cost_estimate=cost(2 * tokens * 3 * q.shape[1] * tokens * 2, 12 * tokens * q.shape[1]),
        compiler_params=PARAMS,
        name="rest",
    )(q, g, far, near, *[x for part in parts for x in part])


def final_call(own, far, near, key_grad, value_grad):
    return pl.pallas_call(
        functools.partial(final_kernel, key_grad.shape[0]),
        in_specs=[ON_CHIP] * 3 + [IN_HBM] * 2,
        out_specs=[IN_HBM] * 2,
        out_shape=[bf16(*key_grad.shape)] * 2,
        scratch_shapes=[pltpu.VMEM(own.shape, jnp.bfloat16), pltpu.SemaphoreType.DMA((2,))],
        input_output_aliases={3: 0, 4: 1},
        cost_estimate=cost(0, 16 * own.shape[0] * own.shape[1]),
        compiler_params=PARAMS,
        name="final",
    )(own, far, near, key_grad, value_grad)


def shards(queries, key_states, value_states, out_grad, segment_ids):
    tokens = queries.shape[0]
    group = queries.shape[1] // (HK * HD)
    scale = HD ** (-0.5)
    chunks = range(CHUNKS)
    step = HK // CHUNKS
    own = [pack_call(key_states, value_states, segment_ids)]
    q, g, qt, gt, later = turn_call(queries, out_grad, key_states, value_states, group)
    own.append(later)
    two = [shift(x, 2) for x in own]
    one = [shift(x, 1) for x in own]
    first, near, far, bias = [], [], [], None
    for c in chunks:
        results = score_call(q, g, qt, gt, own[c], two[c], one[c], bias, c * step, group, tokens, scale)
        bias = results[4] if bias is None else bias
        first.append(results)
        far.append(shift(results[2], -2))
        near.append(shift(results[3], -1))
    query_grad, key_grad, value_grad, own_terms = rest_call(
        q, g, far[0], near[0], [(first[c][0], first[c][1], own[c], two[c], one[c]) for c in chunks],
        group, tokens, scale,
    )
    key_grad, value_grad = final_call(own_terms, far[1], near[1], key_grad, value_grad)
    return query_grad, key_grad, value_grad


def solution(mesh):
    rows = P(AXES, None)
    return jax.shard_map(
        shards,
        mesh=mesh,
        in_specs=(rows, rows, rows, rows, P(AXES)),
        out_specs=(rows, rows, rows),
        check_vma=False,
    )
```
